128 devices in a mesh: dom: 64 (over z, x, y), feat: 2 (over core).
Axes of the slice: x: 4, y: 4, z: 4, core: 2. Of those that a mesh axis runs over, the one named last changes fastest.
Arguments:
- features: bfloat16 [98304, 256], P('dom', 'feat'), may hold values from -6 to 6
- tile_weights: bfloat16 [40960, 128, 128], P('dom')
- tile_rows: int32 [40960], P('dom'), may hold values from 0 to 11, as said below
- tile_slots: int32 [40960], P('dom'), may hold values from 0 to 139, as said below
- send_blocks: int32 [64, 64, 2], P('dom'), may hold values from 0 to 11, as said below
- weight: bfloat16 [256, 256], replicated, may hold values from -0.375 to 0.375
- cotangent: bfloat16 [98304, 256], P(('dom', 'feat')), may hold values from -6 to 6
Outputs:
- hidden: bfloat16 [98304, 256], P(('dom', 'feat'))
- grad_features: bfloat16 [98304, 256], P('dom', 'feat')
- grad_weight: float32 [256, 256], P('feat')
The draws below stay inside these ranges and needn't reach their ends.
Inputs may be any that keep to these rules, and one draw needn't show every extreme that they name: Within each partition tile_rows never falls; the first tile is in row block 0 and the last in row block 11. `tile_slots`: A partition never uses the slots of its own range 12 + d * 2 ...; from peer p it uses the first few of its 2 slots, and every used slot appears in some tile. Each partition reads exactly 2 blocks from the partition before it. `send_blocks`: local block indices of the owner, distinct within each owner and reader pair; every slot names a block, used or not.
All inputs are finite; a program needn't handle non-finite values.
Results may differ from the reference program's by a relative error of at most 0.0067.
Values may be sent and summed in bfloat16 or wider, within the bound.
A program may use at most 256 MiB of HBM per device.

```python
import jax
import jax.numpy as jnp
from jax import lax

BLK = 128
F = 256
HID = 256
NB_DEV = 12
TILE_DEV = 640
CAP = 2
NODES = 98304
TILES = 40960
N_DOM = 64


def draw_tile_weights(key, part):
    key = jax.random.fold_in(key, 11)
    first_key, second_key = jax.random.split(key, 2)
    shape = (TILES, BLK, BLK)
    density = max(0.02, 2.0 / BLK)
    present = (jax.random.randint(first_key, shape, 0, 10000) < int(density * 10000)).astype(jnp.float32)
    factor = (TILE_DEV * BLK * density / NB_DEV) ** (-0.5)
    values = jax.random.uniform(second_key, shape, jnp.float32, 0.5, 1.5)
    return (present * values * factor).astype(jnp.bfloat16)


def draw_tile_rows(key, part):
    key = jax.random.fold_in(key, 12)
    drawn = jax.random.randint(key, (N_DOM, TILE_DEV), 0, NB_DEV).astype(jnp.int32)
    drawn = jnp.sort(drawn, axis=1)
    drawn = drawn.at[:, 0].set(0).at[:, TILE_DEV - 1].set(NB_DEV - 1)
    return drawn.reshape(-1).astype(jnp.int32)


def draw_tile_slots(key, part):
    key = jax.random.fold_in(key, 13)
    first_key, second_key = jax.random.split(key)
    slot_total = NB_DEV + N_DOM * CAP
    filled = jax.random.randint(first_key, (N_DOM, N_DOM), 0, CAP + 1).astype(jnp.int32)
    owners = jnp.arange(N_DOM, dtype=jnp.int32)
    filled = filled.at[owners, (owners + 1) % N_DOM].set(CAP)
    diagonal_mask = owners[:, None] == owners[None, :]
    filled = jnp.where(diagonal_mask, 0, filled)
    positions = jnp.arange(CAP, dtype=jnp.int32)
    remote_used = filled.T[:, :, None] > positions[None, None, :]
    used = jnp.concatenate([jnp.ones((N_DOM, NB_DEV), bool), remote_used.reshape(N_DOM, N_DOM * CAP)], axis=1)
    scores = jax.random.randint(second_key, (N_DOM, slot_total), 0, 1 << 16).astype(jnp.int32)
    ranking = jnp.where(used, scores, 1 << 17) * slot_total + jnp.arange(slot_total, dtype=jnp.int32)[None, :]
    ranked = jnp.argsort(ranking, axis=1).astype(jnp.int32)
    used_count = jnp.sum(used.astype(jnp.int32), axis=1)
    picks = jnp.arange(TILE_DEV, dtype=jnp.int32)[None, :] % used_count[:, None]
    chosen = jnp.take_along_axis(ranked, picks, axis=1)
    return chosen.reshape(-1).astype(jnp.int32)


def draw_send_blocks(key, part):
    key = jax.random.fold_in(key, 14)
    scores = jax.random.randint(key, (N_DOM, N_DOM, NB_DEV), 1, (1 << 16) + 1).astype(jnp.int32)
    owners = jnp.arange(N_DOM, dtype=jnp.int32)
    scores = scores.at[owners, (owners + 1) % N_DOM, NB_DEV - 1].set(0)
    scores = scores.at[owners, (owners + 2) % N_DOM, 0].set(0)
    ranking = scores * NB_DEV + jnp.arange(NB_DEV, dtype=jnp.int32)
    ranked = jnp.argsort(ranking, axis=-1).astype(jnp.int32)
    return ranked[:, :, :CAP].astype(jnp.int32)


def steps_of(rng, dims, cuts, smallest, high):
    level, own = 1.0, jax.random.fold_in(rng, 6)
    for dim, parts in cuts:
        steps = jnp.exp(jax.random.uniform(jax.random.fold_in(own, dim), (parts,), jnp.float32, smallest / len(cuts), high / len(cuts)))
        level = level * jnp.repeat(steps, dims[dim] // parts).reshape([-1 if axis == dim else 1 for axis in range(len(dims))])
    return level


def normal_values(own_key, extent, width, bound, pieces=(), held_as=jnp.bfloat16):
    loudness = steps_of(own_key, extent, pieces, -0.22, 0.18) if pieces else 1.0
    array = jax.random.normal(own_key, extent, jnp.float32) * width * loudness
    return jnp.minimum(jnp.maximum(array, -bound), bound).astype(held_as)


def setup_inputs(seed: int = 0) -> dict:
    streams_of = jax.random.split(jax.random.key(seed), 8)
    return {
        "features": normal_values(streams_of[0], (NODES, F), 1.0, 6.0, ((0, 64), (1, 2))),
        "tile_weights": draw_tile_weights(jax.random.fold_in(streams_of[7], 71), 0),
        "tile_rows": draw_tile_rows(jax.random.fold_in(streams_of[7], 71), 0),
        "tile_slots": draw_tile_slots(jax.random.fold_in(streams_of[7], 71), 0),
        "send_blocks": draw_send_blocks(jax.random.fold_in(streams_of[7], 71), 0),
        "weight": normal_values(streams_of[5], (F, HID), F ** -0.5, 0.375),
        "cotangent": normal_values(streams_of[6], (NODES, HID), 1.0, 6.0, ((0, 128),)),
    }


def reference(features, tile_weights, tile_rows, tile_slots, send_blocks, weight, cotangent):
    slot_total = NB_DEV + N_DOM * CAP
    node_blocks = features.reshape(N_DOM * NB_DEV, BLK, F)
    tile_blocks = tile_weights.reshape(N_DOM, TILE_DEV, BLK, BLK)
    row_lists = tile_rows.reshape(N_DOM, TILE_DEV)
    slot_lists = tile_slots.reshape(N_DOM, TILE_DEV)

    def columns(part_index, slot):
        beyond = jnp.maximum(slot - NB_DEV, 0)
        peer_index = beyond // CAP
        position = beyond % CAP
        remote = peer_index * NB_DEV + send_blocks[peer_index, part_index, position]
        return jnp.where(slot < NB_DEV, part_index * NB_DEV + slot, remote).astype(jnp.int32)

    def forward_part(part_index):
        sources = columns(part_index, slot_lists[part_index])
        products = jnp.einsum("tij,tjf->tif", tile_blocks[part_index].astype(jnp.float32), node_blocks[sources].astype(jnp.float32))
        return jax.ops.segment_sum(products, row_lists[part_index], num_segments=NB_DEV)

    summed = lax.map(forward_part, jnp.arange(N_DOM, dtype=jnp.int32))
    aggregated = summed.astype(jnp.bfloat16).reshape(NODES, F)
    pre = jnp.dot(aggregated, weight, preferred_element_type=jnp.float32)
    hidden = jax.nn.silu(pre).astype(jnp.bfloat16)
    sigmoid_pre = jax.nn.sigmoid(pre)
    slope = sigmoid_pre * (1.0 + pre * (1.0 - sigmoid_pre))
    grad_pre = (cotangent.astype(jnp.float32) * slope).astype(jnp.bfloat16)
    grad_weight = jnp.dot(aggregated.T, grad_pre, preferred_element_type=jnp.float32) * (NODES ** -0.5)
    grad_cols = jnp.dot(grad_pre, weight.T, preferred_element_type=jnp.float32).astype(jnp.bfloat16)
    grad_cols = grad_cols.reshape(N_DOM, NB_DEV, BLK, F)

    def backward_part(running, part_index):
        gathered = grad_cols[part_index][row_lists[part_index]].astype(jnp.float32)
        back_terms = jnp.einsum("tji,tjf->tif", tile_blocks[part_index].astype(jnp.float32), gathered)
        per_slot = jax.ops.segment_sum(back_terms, slot_lists[part_index], num_segments=slot_total)
        own_index = part_index * NB_DEV + jnp.arange(NB_DEV, dtype=jnp.int32)
        running = running.at[own_index].add(per_slot[:NB_DEV])
        remote = lax.optimization_barrier(per_slot[NB_DEV:].astype(jnp.bfloat16)).astype(per_slot.dtype)
        remote_index = (jnp.arange(N_DOM, dtype=jnp.int32)[:, None] * NB_DEV + send_blocks[:, part_index, :]).reshape(-1)
        running = running.at[remote_index].add(remote)
        return running, None

    running = jnp.zeros((N_DOM * NB_DEV, BLK, F), jnp.float32)
    running, _ = lax.scan(backward_part, running, jnp.arange(N_DOM, dtype=jnp.int32))
    grad_features = running.astype(jnp.bfloat16).reshape(NODES, F)
    return hidden, grad_features, grad_weight
```

```python
import functools

import jax
import jax.numpy as jnp
from jax import lax
from jax.experimental import pallas as pl
from jax.experimental.pallas import tpu as pltpu
from jax.sharding import PartitionSpec as P

MESH = pl.DeviceIdType.MESH
F32, BF16, I32 = jnp.float32, jnp.bfloat16, jnp.int32

BLK = 128
NB = 12
TILES = 640
SIDE = 4
NVAR = 3
ROWS = (48, 48, 32)
FIRST = (0, 48, 96)

FC, BC = 8, 2
FU = 92
BU = 390
FCH, BCH = 6, 7

X_OWN, X_HOP, X_END, X_SIZE = 1, 16, 144, 240
Y_ONE, Y_TWO, Y_SIZE = 128, 224, 320
RUN_ZERO = BU
OFFS = (1, 3, 2)


def body(
    feats, tiles_hbm, rows_ref, slots_ref, tab_ref, tab_sm, weight, cot,
    hidden, grad_out, gw_out,
    w, x0, x1, x2, y0, y1, y2, ag0, ag1, ag2, v0, v1, v2, rr0, rr1, rr2,
    runs, tabs, tabs_sm, flist, flist_sm, blist, blist_sm, ends, ends_sm, rlist, rlist_sm,
    full, send_a, gt, send_g, wt, wt_in, gw0, gw1, gw2, gw3,
    w_sem, sm_sem, feat_s, feat_r, tab_s, tab_r,
    s1_s, s1_r, s2_s, s2_r, s3_s, s3_r, b3_s, b3_r, b2_s, b2_r, b1_s, b1_r, gw_s, gw_r,
):
    x, y, ag, vin, rr = (x0, x1, x2), (y0, y1, y2), (ag0, ag1, ag2), (v0, v1, v2), (rr0, rr1, rr2)
    dom, feat = lax.axis_index("dom"), lax.axis_index("feat")
    cz, cx, cy = lax.div(dom, 16), lax.rem(lax.div(dom, 4), 4), lax.rem(dom, 4)

    def moved(axis_is_z, axis_is_x, off):
        z = lax.rem(cz + off, 4) * 16 + cx * 4 + cy
        xx = cz * 16 + lax.rem(cx + off, 4) * 4 + cy
        yy = cz * 16 + cx * 4 + lax.rem(cy + off, 4)
        return jnp.where(axis_is_z, z, jnp.where(axis_is_x, xx, yy))

    turn = [lax.rem(v + feat, 3) for v in range(NVAR)]

    def role(v, which):
        axis = lax.rem(turn[v] + which, 3)
        return axis == 0, axis == 1

    def peer(v, which, off):
        return (moved(*role(v, which), off), feat)

    def reader(v, db, dc):
        z, xx, yy = (lax.rem(c + d, 4) for c, d in ((cz, 0), (cx, 0), (cy, 0)))
        t = turn[v]
        z = lax.rem(cz + jnp.where(t == 1, dc, jnp.where(t == 2, db, 0)), 4)
        xx = lax.rem(cx + jnp.where(t == 0, db, jnp.where(t == 2, dc, 0)), 4)
        yy = lax.rem(cy + jnp.where(t == 0, dc, jnp.where(t == 1, db, 0)), 4)
        return z * 16 + xx * 4 + yy

    started = []

    def send(src, dst, ssem, rsem, device):
        cp = pltpu.make_async_remote_copy(
            src_ref=src, dst_ref=dst, send_sem=ssem, recv_sem=rsem, device_id=device, device_id_type=MESH
        )
        cp.start()
        started.append(cp)
        return cp

    other = (dom, 1 - feat)

    barrier = pltpu.get_barrier_semaphore()
    for axis in range(3):
        for off in (1, 2, 3):
            pl.semaphore_signal(
                barrier, inc=1, device_id=(moved(axis == 0, axis == 1, off), feat), device_id_type=MESH
            )
    pl.semaphore_signal(barrier, inc=1, device_id=other, device_id_type=MESH)
    pl.semaphore_wait(barrier, 10)

    tab_cp, s1, s2, s3 = {}, {}, {}, {}
    for v in range(NVAR):
        for off in OFFS:
            i = v * 4 + off
            tab_cp[v, off] = send(tab_ref, tabs.at[v * 4 + (4 - off)], tab_s.at[i], tab_r.at[i], peer(v, 0, off))
    for off in OFFS:
        for v in range(NVAR):
            i = v * 4 + off
            s1[v, off] = send(
                feats.at[:, pl.ds(FIRST[v], ROWS[v])], ag[v].at[pl.ds((4 - off) * NB, NB)],
                s1_s.at[i], s1_r.at[i], peer(v, 0, off),
            )
    w_cp = pltpu.make_async_copy(tiles_hbm, w, w_sem.at[0])
    w_cp.start()

    for v in range(NVAR):
        chunk = pl.ds(FIRST[v], ROWS[v])
        x[v][0] = jnp.zeros((ROWS[v], BLK), BF16)
        for j in range(NB):
            block = feats[j, chunk]
            x[v][X_OWN + j] = block
            ag[v][j] = block
        tabs[v * 4] = tab_ref[...]

    lane = lax.broadcasted_iota(I32, (BLK, BLK), 1)
    sub = lax.broadcasted_iota(I32, (BLK, BLK), 0)
    ones = jnp.ones((BLK, BLK), I32)

    def column(row):
        return jnp.transpose(ones * row)

    def hits(mask):
        return jnp.where(mask, 1, 0)

    chunks = range(TILES // BLK)

    row_r = [rows_ref[pl.ds(c, 1), :] for c in chunks]
    slot_r = [slots_ref[pl.ds(c, 1), :] for c in chunks]
    row_c = [column(r) for r in row_r]
    lane1 = lane[0:1]
    row_count = sum(jnp.sum(hits(r == lane), axis=0, keepdims=True) for r in row_c)
    row_units = lax.shift_right_logical(row_count + (FC - 1), FC.bit_length() - 1)
    row_units_c, row_count_c = column(row_units), column(row_count)
    row_first = jnp.sum(jnp.where(sub < lane, row_units_c, 0), axis=0, keepdims=True)
    row_begin = jnp.sum(jnp.where(sub < lane, row_count_c, 0), axis=0, keepdims=True)
    row_last = jnp.where(row_count > 0, row_first + row_units - 1, RUN_ZERO)
    ends[pl.ds(2, 1), :] = row_last

    def digits(block):
        pz, px, py = lax.shift_right_logical(block, 4), lax.shift_right_logical(block, 2) & 3, block & 3
        return (pz - cz) & 3, (px - cx) & 3, (py - cy) & 3

    def roles(v, rel):
        rz, rx, ry = rel
        t = turn[v]
        first = jnp.where(t == 0, rz, jnp.where(t == 1, rx, ry))
        second = jnp.where(t == 0, rx, jnp.where(t == 1, ry, rz))
        third = jnp.where(t == 0, ry, jnp.where(t == 1, rz, rx))
        return first, second, third

    def x_entry(v, slot):
        far = jnp.maximum(slot - NB, 0)
        k = far & 1
        d, b, g = roles(v, digits(lax.shift_right_logical(far, 1)))
        near = X_HOP + ((b * 4) * 4 + d) * 2 + k
        end = X_END + (((g - 1) * 4 + b) * 4 + d) * 2 + k
        return jnp.where(slot < NB, X_OWN + slot, jnp.where(g == 0, near, end))

    place, tile_c = [], []
    for c in chunks:
        offset = jnp.sum(jnp.where(row_c[c] == lane, FC * row_first - row_begin, 0), axis=1, keepdims=True)
        tile_c.append(sub + c * BLK)
        place.append(offset + tile_c[c])
    for v in range(NVAR):
        entry_c = [column(x_entry(v, s)) for s in slot_r]
        for q in range(FCH):
            at = lane + q * BLK
            found = sum(
                jnp.sum(jnp.where(place[c] == at, entry_c[c], 0), axis=0, keepdims=True) for c in chunks
            )
            flist[pl.ds((v + 1) * 8 + q, 1), :] = found
    for q in range(FCH):
        at = lane + q * BLK
        found = sum(
            jnp.sum(jnp.where(place[c] == at, tile_c[c], 0), axis=0, keepdims=True) for c in chunks
        )
        flist[pl.ds(q, 1), :] = found
        starts = sum(
            jnp.sum(
                jnp.where(
                    (place[c] == at)
                    & (tile_c[c] == jnp.sum(jnp.where(row_c[c] == lane, row_begin, 0), axis=1, keepdims=True)),
                    1, 0,
                ),
                axis=0, keepdims=True,
            )
            for c in chunks
        )
        flist[pl.ds(32 + q, 1), :] = starts

    for v in range(NVAR):
        for off in OFFS:
            tab_cp[v, off].wait_recv()
    tabs_cp = pltpu.make_async_copy(tabs, tabs_sm, sm_sem.at[0])
    tabs_cp.start()
    tabs_cp.wait()

    def pack(v, db, dc, dst, base):
        at = reader(v, db, dc) * 2
        for d in range(4):
            for k in range(2):
                j = tabs_sm[v * 4 + d, 0, at + k]
                dst[base + d * 2 + k] = ag[v][d * NB + j]

    def pass_on(v, b, dc):
        i = (v * 4 + b) * 4 + dc
        s3[v, b, dc] = send(
            x[v].at[pl.ds(X_HOP + (b * 4 + dc) * 8, 8)],
            x[v].at[pl.ds(X_END + ((4 - dc - 1) * 4 + b) * 8, 8)],
            s3_s.at[i], s3_r.at[i], peer(v, 2, dc),
        )

    for v in range(NVAR):
        for off in OFFS:
            s1[v, off].wait_recv()
        for dc in (1, 3, 2, 0):
            pack(v, 0, dc, x[v], X_HOP + dc * 8)
            if dc:
                pass_on(v, 0, dc)
            for db in OFFS:
                base = (db * 4 + dc) * 8
                pack(v, db, dc, y[v], base)
                i = (v * 4 + db) * 4 + dc
                s2[v, db, dc] = send(
                    y[v].at[pl.ds(base, 8)], x[v].at[pl.ds(X_HOP + ((4 - db) * 4 + dc) * 8, 8)],
                    s2_s.at[i], s2_r.at[i], peer(v, 1, db),
                )

    slot_c = [column(s) for s in slot_r]
    counts = [sum(jnp.sum(hits(s == lane + h * BLK), axis=0, keepdims=True) for s in slot_c) for h in range(2)]
    units = [lax.shift_right_logical(n + (BC - 1), BC.bit_length() - 1) for n in counts]
    units_c = [column(u) for u in units]
    firsts = [
        jnp.sum(jnp.where(sub < lane, units_c[0], 0), axis=0, keepdims=True),
        jnp.sum(jnp.where(sub < lane, units_c[1], 0) + units_c[0], axis=0, keepdims=True),
    ]
    for h in range(2):
        last = jnp.where(counts[h] > 0, firsts[h] + units[h] - 1, RUN_ZERO)
        ends[pl.ds(h, 1), :] = last
    order, place = [], []
    for c in chunks:
        before = sum(hits((slot_c[c] == slot_r[e]) & (lane + e * BLK < tile_c[c])) for e in chunks)
        order.append(jnp.sum(before, axis=1, keepdims=True))
        begin = jnp.sum(
            sum(jnp.where(slot_c[c] == lane + h * BLK, firsts[h], 0) for h in range(2)),
            axis=1, keepdims=True,
        )
        place.append(ones * (BC * begin + order[c]))
    start_c = [hits(o == 0) * ones for o in order]
    row_next = [r + 1 for r in row_c]
    for q in range(BCH):
        at = lane + q * BLK
        for base, what in ((0, tile_c), (8, row_next), (16, start_c)):
            found = sum(jnp.sum(jnp.where(place[c] == at, what[c], 0), axis=0, keepdims=True) for c in chunks)
            blist[pl.ds(base + q, 1), :] = found

    index1 = lax.broadcasted_iota(I32, (1, BLK), 1)
    for v in range(NVAR):
        k = index1 & 1
        d, b, g = roles(v, digits(lax.shift_right_logical(index1, 1)))
        own = Y_TWO + ((b - 1) * 4 + g) * 8 + k
        loc = jnp.where(b > 0, own, jnp.where(g > 0, Y_ONE + (g - 1) * 32 + k, k))
        loc_c = column(loc)
        for o in range(4):
            block = jnp.where(d == 0, tabs[v * 4 + o], 64)
            key = block * 128 + lane1
            block_c, key_c = column(block), column(key)
            rank = jnp.sum(hits(key_c < key), axis=0, keepdims=True)
            begin = jnp.sum(hits(block_c < block), axis=0, keepdims=True)
            rank_c, begin_c = column(rank), column(begin)
            value = loc_c + o * 2 + 512 * hits(rank_c == begin_c)
            found = jnp.sum(jnp.where(rank_c == lane, value, 0), axis=0, keepdims=True)
            upto = jnp.sum(hits(block_c <= lane), axis=0, keepdims=True)
            count = jnp.sum(hits(block_c == lane), axis=0, keepdims=True)
            rlist[pl.ds((v * 4 + o) * 2, 1), :] = found
            rlist[pl.ds((v * 4 + o) * 2 + 1, 1), :] = jnp.where(count > 0, upto - 1, 32)

    to_sm = [
        pltpu.make_async_copy(a, b, sm_sem.at[1 + i])
        for i, (a, b) in enumerate(((flist, flist_sm), (blist, blist_sm), (ends, ends_sm), (rlist, rlist_sm)))
    ]
    for cp in to_sm:
        cp.start()

    for v in range(NVAR):
        for dc in (1, 3, 2, 0):
            for db in OFFS:
                s2[v, db, dc].wait_recv()
                if dc:
                    pass_on(v, 4 - db, dc)
    runs[RUN_ZERO] = jnp.zeros((BLK, BLK), BF16)
    gt[0] = jnp.zeros((BLK, BLK), BF16)
    for cp in to_sm:
        cp.wait()
    for v in range(NVAR):
        for b in (0, 3, 1, 2):
            for dc in OFFS:
                s3[v, b, dc].wait_recv()
    w_cp.wait()

    def forward_unit(u, acc):
        r, q = lax.div(u, 16), lax.rem(u, 16) * FC
        left, right = [], []
        for i in range(FC):
            left.append(w[flist_sm[r, q + i]])
            for v in range(NVAR):
                right.append(x[v][flist_sm[(v + 1) * 8 + r, q + i]])
        got = jnp.dot(
            jnp.concatenate(left, axis=1), jnp.concatenate(right, axis=0), preferred_element_type=F32
        )
        acc = jnp.where(flist_sm[32 + r, q] > 0, 0.0, acc) + got
        runs[u] = acc.astype(BF16)
        return acc

    lax.fori_loop(0, FU, forward_unit, jnp.zeros((BLK, BLK), F32), unroll=2)

    half = NB // 2
    mine, theirs = feat * half, (1 - feat) * half
    for i in range(half):
        send_a[i] = runs[ends_sm[2, theirs + i]]
    cp_a = send(send_a, full.at[feat], feat_s.at[0], feat_r.at[0], other)
    for i in range(half):
        full[feat, i] = runs[ends_sm[2, mine + i]]
    cp_a.wait_recv()

    wt[...] = jnp.zeros_like(wt)
    cp_g = []
    for i in range(half):
        left, right = full[0, i], full[1, i]
        pre = jnp.dot(left, weight[0:BLK, :], preferred_element_type=F32)
        pre += jnp.dot(right, weight[BLK:, :], preferred_element_type=F32)
        sig = jax.nn.sigmoid(pre)
        nodes = pl.ds(i * BLK, BLK)
        hidden[nodes, :] = (pre * sig).astype(BF16)
        grad = (cot[nodes, :].astype(F32) * (sig * (1.0 + pre * (1.0 - sig)))).astype(BF16)
        send_g[i] = lax.dot_general(
            weight[pl.ds((1 - feat) * BLK, BLK), :], grad, (((1,), (1,)), ((), ())), preferred_element_type=F32
        ).astype(BF16)
        cp = send(send_g.at[i], gt.at[1 + mine + i], feat_s.at[1 + i], feat_r.at[1 + i], other)
        cp_g.append(cp)
        gt[1 + mine + i] = lax.dot_general(
            weight[pl.ds(feat * BLK, BLK), :], grad, (((1,), (1,)), ((), ())), preferred_element_type=F32
        ).astype(BF16)
        for h, part in ((0, left), (1, right)):
            wt[h] += lax.dot_general(part, grad, (((0,), (0,)), ((), ())), preferred_element_type=F32)
    cp_w = send(wt.at[1 - feat], wt_in, feat_s.at[7], feat_r.at[7], other)
    for cp in cp_g:
        cp.wait_recv()

    def backward_unit(u, acc):
        r, q = lax.div(u, 64), lax.rem(u, 64) * BC
        left = [gt[blist_sm[8 + r, q + i]] for i in range(BC)]
        right = [w[blist_sm[r, q + i]] for i in range(BC)]
        got = jnp.dot(
            jnp.concatenate(left, axis=1), jnp.concatenate(right, axis=0), preferred_element_type=F32
        )
        acc = jnp.where(blist_sm[16 + r, q] > 0, 0.0, acc) + got
        runs[u] = acc.astype(BF16)
        return acc

    lax.fori_loop(0, BU, backward_unit, jnp.zeros((BLK, BLK), F32), unroll=6)

    packed = list(s2.values())
    for cp in packed:
        cp.wait_send()
    b3, b2, b1 = {}, {}, {}

    def fill(v, g, b):
        for d in range(4):
            t = turn[v]
            z = lax.rem(cz + jnp.where(t == 0, d, jnp.where(t == 1, g, b)), 4)
            xx = lax.rem(cx + jnp.where(t == 0, b, jnp.where(t == 1, d, g)), 4)
            yy = lax.rem(cy + jnp.where(t == 0, g, jnp.where(t == 1, b, d)), 4)
            slot = NB + (z * 16 + xx * 4 + yy) * 2
            for k in range(2):
                s = slot + k
                run = ends_sm[lax.div(s, BLK), lax.rem(s, BLK)]
                y[v][(g * 4 + b) * 8 + d * 2 + k] = runs[run, pl.ds(FIRST[v], ROWS[v])]

    def go_back(v, lam, kap):
        src = y[v].at[pl.ds(lam * 8, 8)] if kap == 0 else y[v].at[pl.ds(Y_ONE + ((kap - 1) * 4 + lam) * 8, 8)]
        i = (v * 4 + lam) * 4 + kap
        b2[v, lam, kap] = send(
            src, y[v].at[pl.ds(Y_TWO + ((4 - lam - 1) * 4 + kap) * 8, 8)],
            b2_s.at[i], b2_r.at[i], peer(v, 1, lam),
        )

    for b in (1, 3, 2, 0):
        for v in range(NVAR):
            for g in OFFS:
                fill(v, g, b)
                i = (v * 4 + g) * 4 + b
                b3[v, g, b] = send(
                    y[v].at[pl.ds((g * 4 + b) * 8, 8)],
                    y[v].at[pl.ds(Y_ONE + ((4 - g - 1) * 4 + b) * 8, 8)],
                    b3_s.at[i], b3_r.at[i], peer(v, 2, g),
                )
            fill(v, 0, b)
            if b:
                go_back(v, b, 0)

    cp_w.wait_recv()
    wt[feat] = wt[feat] + wt_in[...]
    gz, gx, gy = [], [], []

    def gw_copy(store, n, src, dst, axis, off):
        cp = send(src, dst, gw_s.at[n], gw_r.at[n], (moved(axis == 0, axis == 1, off), feat))
        store.append(cp)

    for off in OFFS:
        to = lax.rem(cz + off, 4)
        gw_copy(gz, off, wt.at[feat, pl.ds(to * 32, 32)], gw0.at[off], 0, off)

    for b in (1, 3, 2):
        for v in range(NVAR):
            for g in OFFS:
                b3[v, g, b].wait_recv()
                go_back(v, b, 4 - g)
        if b == 1:
            for cp in gz:
                cp.wait_recv()
            gw0[0] = wt[feat, pl.ds(cz * 32, 32)] + gw0[1] + gw0[2] + gw0[3]
            for off in OFFS:
                to = lax.rem(cx + off, 4)
                gw_copy(gx, 4 + off, gw0.at[0, pl.ds(to * 8, 8)], gw1.at[off], 1, off)
        if b == 3:
            for cp in gx:
                cp.wait_recv()
            gw2[cy] = gw0[0, pl.ds(cx * 8, 8)] + gw1[1] + gw1[2] + gw1[3]
            for off in OFFS:
                gw_copy(gy, 8 + off, gw2.at[cy], gw2.at[cy], 2, off)
    for cp in gy:
        cp.wait_recv()
    scale = float(64 * NB * BLK) ** (-0.5)
    gx2, gz2 = [], []
    gw3[cz, pl.ds(cx * 8, 8)] = (gw2[0] + gw2[1] + gw2[2] + gw2[3]) * scale
    for off in OFFS:
        gw_copy(gx2, 12 + off, gw3.at[cz, pl.ds(cx * 8, 8)], gw3.at[cz, pl.ds(cx * 8, 8)], 1, off)

    runs_r = runs

    for v in range(NVAR):
        for g in OFFS:
            b3[v, g, 0].wait_recv()
    for v in range(NVAR):
        n = ROWS[v]
        for lam in OFFS:
            for kap in range(4):
                b2[v, lam, kap].wait_recv()
        for o in (1, 3, 2, 0):
            r = (v * 4 + o) * 2

            def add(q, acc, v=v, r=r):
                code = rlist_sm[r, q]
                acc = jnp.where(code >= 512, 0.0, acc) + y[v][jnp.minimum(code & 511, Y_SIZE - 1)].astype(F32)
                rr[v][q] = acc.astype(BF16)
                return acc

            lax.fori_loop(0, 32, add, jnp.zeros((n, BLK), F32), unroll=4)
            rr[v][32] = jnp.zeros((n, BLK), BF16)
            for j in range(NB):
                ag[v][o * NB + j] = rr[v][rlist_sm[r + 1, j]]
            if o:
                i = v * 4 + o
                b1[v, o] = send(
                    ag[v].at[pl.ds(o * NB, NB)], vin[v].at[pl.ds((4 - o - 1) * NB, NB)],
                    b1_s.at[i], b1_r.at[i], peer(v, 0, o),
                )

    for cp in gx2:
        cp.wait_recv()
    for off in OFFS:
        gw_copy(gz2, off + 16, gw3.at[cz], gw3.at[cz], 0, off)

    for v in range(NVAR):
        for off in OFFS:
            b1[v, off].wait_recv()
    for j in range(NB):
        run = ends_sm[0, j]
        parts = []
        for v in range(NVAR):
            total = runs[run, pl.ds(FIRST[v], ROWS[v])].astype(F32) + ag[v][j].astype(F32)
            for off in range(3):
                total += vin[v][off * NB + j].astype(F32)
            parts.append(total)
        grad_out[pl.ds(j * BLK, BLK), :] = jnp.transpose(jnp.concatenate(parts, axis=0)).astype(BF16)

    for cp in gz2:
        cp.wait_recv()
    for z in range(4):
        gw_out[pl.ds(z * 32, 32), :] = gw3[z]

    for cp in started:
        if not any(cp is p for p in packed):
            cp.wait_send()


def local(features, tile_weights, tile_rows, tile_slots, send_blocks, weight, cotangent):
    dma = lambda n: pltpu.SemaphoreType.DMA((n,))
    vmem = lambda *shape, dtype=BF16: pltpu.VMEM(shape, dtype)
    smem = lambda *shape: pltpu.SMEM(shape, I32)
    in_vmem = pl.BlockSpec(memory_space=pltpu.VMEM)
    table = send_blocks.reshape(1, BLK)
    nodes = NB * BLK
    scratch = [
        vmem(TILES, BLK, BLK),
        *[vmem(X_SIZE, n, BLK) for n in ROWS],
        *[vmem(Y_SIZE, n, BLK) for n in ROWS],
        *[vmem(4 * NB, n, BLK) for n in ROWS],
        *[vmem(3 * NB, n, BLK) for n in ROWS],
        *[vmem(33, n, BLK) for n in ROWS],
        vmem(BU + 1, BLK, BLK),
        vmem(12, 1, BLK, dtype=I32), smem(12, 1, BLK),
        vmem(40, BLK, dtype=I32), smem(40, BLK),
        vmem(24, BLK, dtype=I32), smem(24, BLK),
        vmem(8, BLK, dtype=I32), smem(8, BLK),
        vmem(24, BLK, dtype=I32), smem(24, BLK),
        vmem(2, NB // 2, BLK, BLK), vmem(NB // 2, BLK, BLK), vmem(NB + 1, BLK, BLK), vmem(NB // 2, BLK, BLK),
        vmem(2, BLK, 256, dtype=F32), vmem(BLK, 256, dtype=F32),
        vmem(4, 32, 256, dtype=F32), vmem(4, 8, 256, dtype=F32), vmem(4, 8, 256, dtype=F32),
        vmem(4, 32, 256, dtype=F32),
        dma(1), dma(5), dma(8), dma(8), dma(12), dma(12),
        dma(12), dma(12), dma(48), dma(48), dma(48), dma(48),
        dma(48), dma(48), dma(48), dma(48), dma(12), dma(12), dma(20), dma(20),
    ]
    return pl.pallas_call(
        body,
        out_shape=(
            jax.ShapeDtypeStruct((nodes // 2, 256), BF16),
            jax.ShapeDtypeStruct((nodes, BLK), BF16),
            jax.ShapeDtypeStruct((BLK, 256), F32),
        ),
        in_specs=[
            in_vmem, pl.BlockSpec(memory_space=pl.ANY), in_vmem, in_vmem, in_vmem,
            pl.BlockSpec(memory_space=pltpu.SMEM), in_vmem, in_vmem,
        ],
        out_specs=(in_vmem, in_vmem, in_vmem),
        scratch_shapes=scratch,
        compiler_params=pltpu.CompilerParams(
            collective_id=0, has_side_effects=True, vmem_limit_bytes=64 * 2**20 - 2**16
        ),
        cost_estimate=pl.CostEstimate(flops=6 * 10**9, bytes_accessed=24 * 2**20, transcendentals=400000),
    )(
        features.reshape(NB, BLK, BLK), tile_weights, tile_rows.reshape(5, BLK), tile_slots.reshape(5, BLK),
        table, table, weight, cotangent,
    )


def solution(mesh):
    placed = (
        P("dom", "feat"),
        P("dom", None, None),
        P("dom"),
        P("dom"),
        P("dom", None, None),
        P(),
        P(("dom", "feat"), None),
    )
    return jax.shard_map(
        local,
        mesh=mesh,
        in_specs=placed,
        out_specs=(P(("dom", "feat"), None), P("dom", "feat"), P("feat", None)),
        check_vma=False,
    )
```

```python
import functools

import jax
import jax.numpy as jnp
from jax import lax
from jax.experimental import pallas as pl
from jax.experimental.pallas import tpu as pltpu
from jax.sharding import PartitionSpec as P

MESH = pl.DeviceIdType.MESH
F32, BF16, I32 = jnp.float32, jnp.bfloat16, jnp.int32

BLK = 128
NB = 12
TILES = 640
SIDE = 4
NVAR = 3
ROWS = (48, 48, 32)
FIRST = (0, 48, 96)

FC, BC = 8, 2
FU = 96
BU = 390
FCH, BCH = 6, 7

X_OWN, X_HOP, X_END, X_SIZE = 1, 16, 144, 240
Y_ONE, Y_TWO, Y_SIZE = 128, 224, 320
RUN_ZERO = BU
OFFS = (1, 3, 2)


def body(
    feats, tiles_hbm, rows_ref, slots_ref, tab_in, weight_hbm, cot_hbm,
    hidden_hbm, grad_out, gw_out,
    w, x0, x1, x2, y0, y1, y2, ag0, ag1, ag2, v0, v1, v2, rr0, rr1, rr2,
    runs, tabs, tabs_sm, flist, flist_sm, blist, blist_sm, ends, ends_sm, rlist, rlist_sm,
    weight, cot, hidden, tab_ref, full, send_a, gt, send_g, wt, wt_in, gw0, gw1, gw2, gw3,
    in_sem, sm_sem, feat_s, feat_r, tab_s, tab_r,
    s1_s, s1_r, s2_s, s2_r, s3_s, s3_r, b3_s, b3_r, b2_s, b2_r, b1_s, b1_r, gw_s, gw_r,
):
    x, y, ag, vin, rr = (x0, x1, x2), (y0, y1, y2), (ag0, ag1, ag2), (v0, v1, v2), (rr0, rr1, rr2)
    dom, feat = lax.axis_index("dom"), lax.axis_index("feat")
    cz, cx, cy = lax.div(dom, 16), lax.rem(lax.div(dom, 4), 4), lax.rem(dom, 4)

    def moved(axis_is_z, axis_is_x, off):
        z = lax.rem(cz + off, 4) * 16 + cx * 4 + cy
        xx = cz * 16 + lax.rem(cx + off, 4) * 4 + cy
        yy = cz * 16 + cx * 4 + lax.rem(cy + off, 4)
        return jnp.where(axis_is_z, z, jnp.where(axis_is_x, xx, yy))

    turn = [lax.rem(v + feat, 3) for v in range(NVAR)]

    def role(v, which):
        axis = lax.rem(turn[v] + which, 3)
        return axis == 0, axis == 1

    def peer(v, which, off):
        return (moved(*role(v, which), off), feat)

    def reader(v, db, dc):
        z, xx, yy = (lax.rem(c + d, 4) for c, d in ((cz, 0), (cx, 0), (cy, 0)))
        t = turn[v]
        z = lax.rem(cz + jnp.where(t == 1, dc, jnp.where(t == 2, db, 0)), 4)
        xx = lax.rem(cx + jnp.where(t == 0, db, jnp.where(t == 2, dc, 0)), 4)
        yy = lax.rem(cy + jnp.where(t == 0, dc, jnp.where(t == 1, db, 0)), 4)
        return z * 16 + xx * 4 + yy

    def send(src, dst, ssem, rsem, device):
        cp = pltpu.make_async_remote_copy(
            src_ref=src, dst_ref=dst, send_sem=ssem, recv_sem=rsem, device_id=device, device_id_type=MESH
        )
        cp.start()
        return cp

    def await_arrival(ref, sem):
        pltpu.make_async_copy(ref, ref, sem).wait()

    other = (dom, 1 - feat)

    barrier = pltpu.get_barrier_semaphore()
    for axis in range(3):
        for off in (1, 2, 3):
            pl.semaphore_signal(
                barrier, inc=1, device_id=(moved(axis == 0, axis == 1, off), feat), device_id_type=MESH
            )
    pl.semaphore_signal(barrier, inc=1, device_id=other, device_id_type=MESH)
    pl.semaphore_wait(barrier, 10)

    tab_ref[...] = jnp.concatenate([tab_in[0:1, :], tab_in[1:2, :]], axis=1)
    for v in range(NVAR):
        for off in OFFS:
            send(tab_ref, tabs.at[v * 4 + (4 - off)], tab_s.at[0], tab_r.at[0], peer(v, 0, off))
    for off in OFFS:
        for v in range(NVAR):
            send(
                feats.at[:, pl.ds(FIRST[v], ROWS[v])], ag[v].at[pl.ds((4 - off) * NB, NB)],
                s1_s.at[v], s1_r.at[v], peer(v, 0, off),
            )
    loads = [
        pltpu.make_async_copy(a, b, in_sem.at[i])
        for i, (a, b) in enumerate(((weight_hbm, weight), (cot_hbm, cot), (tiles_hbm, w)))
    ]
    for cp in loads:
        cp.start()

    for v in range(NVAR):
        chunk = pl.ds(FIRST[v], ROWS[v])
        x[v][0] = jnp.zeros((ROWS[v], BLK), BF16)
        for j in range(NB):
            block = feats[j, chunk]
            x[v][X_OWN + j] = block
            ag[v][j] = block
        tabs[v * 4] = tab_ref[...]

    lane = lax.broadcasted_iota(I32, (BLK, BLK), 1)
    sub = lax.broadcasted_iota(I32, (BLK, BLK), 0)
    ones = jnp.ones((BLK, BLK), I32)

    def column(row):
        return jnp.transpose(ones * row)

    def hits(mask):
        return jnp.where(mask, 1, 0)

    chunks = range(TILES // BLK)

    row_r = [rows_ref[pl.ds(c, 1), :] for c in chunks]
    slot_r = [slots_ref[pl.ds(c, 1), :] for c in chunks]
    row_c = [column(r) for r in row_r]
    lane1 = lane[0:1]
    row_count = sum(jnp.sum(hits(r == lane), axis=0, keepdims=True) for r in row_c)
    row_units = lax.shift_right_logical(row_count + (FC - 1), FC.bit_length() - 1)
    row_units_c, row_count_c = column(row_units), column(row_count)
    row_first = jnp.sum(jnp.where(sub < lane, row_units_c, 0), axis=0, keepdims=True)
    row_begin = jnp.sum(jnp.where(sub < lane, row_count_c, 0), axis=0, keepdims=True)
    row_last = jnp.where(row_count > 0, row_first + row_units - 1, RUN_ZERO)
    ends[pl.ds(2, 1), :] = row_last

    def digits(block):
        pz, px, py = lax.shift_right_logical(block, 4), lax.shift_right_logical(block, 2) & 3, block & 3
        return (pz - cz) & 3, (px - cx) & 3, (py - cy) & 3

    def roles(v, rel):
        rz, rx, ry = rel
        t = turn[v]
        first = jnp.where(t == 0, rz, jnp.where(t == 1, rx, ry))
        second = jnp.where(t == 0, rx, jnp.where(t == 1, ry, rz))
        third = jnp.where(t == 0, ry, jnp.where(t == 1, rz, rx))
        return first, second, third

    def x_entry(v, slot):
        far = jnp.maximum(slot - NB, 0)
        k = far & 1
        d, b, g = roles(v, digits(lax.shift_right_logical(far, 1)))
        near = X_HOP + b * 8 + d * 2 + k
        end = X_END + (((g - 1) * 4 + b) * 4 + d) * 2 + k
        return jnp.where(slot < NB, X_OWN + slot, jnp.where(g == 0, near, end))

    place, tile_c = [], []
    for c in chunks:
        offset = jnp.sum(jnp.where(row_c[c] == lane, FC * row_first - row_begin, 0), axis=1, keepdims=True)
        tile_c.append(sub + c * BLK)
        place.append(offset + tile_c[c])
    for v in range(NVAR):
        entry_c = [column(x_entry(v, s)) for s in slot_r]
        for q in range(FCH):
            at = lane + q * BLK
            found = sum(
                jnp.sum(jnp.where(place[c] == at, entry_c[c], 0), axis=0, keepdims=True) for c in chunks
            )
            flist[pl.ds((v + 1) * 8 + q, 1), :] = found
    for q in range(FCH):
        at = lane + q * BLK
        found = sum(
            jnp.sum(jnp.where(place[c] == at, tile_c[c], 0), axis=0, keepdims=True) for c in chunks
        )
        flist[pl.ds(q, 1), :] = found
        starts = sum(
            jnp.sum(
                jnp.where(
                    (place[c] == at)
                    & (tile_c[c] == jnp.sum(jnp.where(row_c[c] == lane, row_begin, 0), axis=1, keepdims=True)),
                    1, 0,
                ),
                axis=0, keepdims=True,
            )
            for c in chunks
        )
        flist[pl.ds(32 + q, 1), :] = starts

    await_arrival(tabs.at[pl.ds(0, 9)], tab_r.at[0])
    tabs_cp = pltpu.make_async_copy(tabs, tabs_sm, sm_sem.at[0])
    tabs_cp.start()
    tabs_cp.wait()

    def pack(v, db, dc, dst, base):
        at = reader(v, db, dc)
        for d in range(4):
            for k in range(2):
                j = tabs_sm[v * 4 + d, 0, at + k * 64]
                dst[base + d * 2 + k] = ag[v][d * NB + j]

    def pass_on(v, b, dc):
        send(
            x[v].at[pl.ds(X_HOP + (dc * 4 + b) * 8, 8)],
            x[v].at[pl.ds(X_END + ((4 - dc - 1) * 4 + b) * 8, 8)],
            s3_s.at[v], s3_r.at[v], peer(v, 2, dc),
        )

    for v in range(NVAR):
        await_arrival(ag[v].at[pl.ds(NB, 3 * NB)], s1_r.at[v])
        for dc in (1, 3, 2, 0):
            pack(v, 0, dc, x[v], X_HOP + dc * 32)
            if dc:
                pass_on(v, 0, dc)
            for db in OFFS:
                base = (db * 4 + dc) * 8
                pack(v, db, dc, y[v], base)
                send(
                    y[v].at[pl.ds(base, 8)], x[v].at[pl.ds(X_HOP + (dc * 4 + (4 - db)) * 8, 8)],
                    s2_s.at[v], s2_r.at[v * 4 + dc], peer(v, 1, db),
                )

    slot_c = [column(s) for s in slot_r]
    counts = [sum(jnp.sum(hits(s == lane + h * BLK), axis=0, keepdims=True) for s in slot_c) for h in range(2)]
    units = [lax.shift_right_logical(n + (BC - 1), BC.bit_length() - 1) for n in counts]
    units_c = [column(u) for u in units]
    firsts = [
        jnp.sum(jnp.where(sub < lane, units_c[0], 0), axis=0, keepdims=True),
        jnp.sum(jnp.where(sub < lane, units_c[1], 0) + units_c[0], axis=0, keepdims=True),
    ]
    for h in range(2):
        last = jnp.where(counts[h] > 0, firsts[h] + units[h] - 1, RUN_ZERO)
        ends[pl.ds(h, 1), :] = last
    order, place = [], []
    for c in chunks:
        before = sum(hits((slot_c[c] == slot_r[e]) & (lane + e * BLK < tile_c[c])) for e in chunks)
        order.append(jnp.sum(before, axis=1, keepdims=True))
        begin = jnp.sum(
            sum(jnp.where(slot_c[c] == lane + h * BLK, firsts[h], 0) for h in range(2)),
            axis=1, keepdims=True,
        )
        place.append(ones * (BC * begin + order[c]))
    start_c = [hits(o == 0) * ones for o in order]
    row_next = [r + 1 for r in row_c]
    for q in range(BCH):
        at = lane + q * BLK
        for base, what in ((0, tile_c), (8, row_next), (16, start_c)):
            found = sum(jnp.sum(jnp.where(place[c] == at, what[c], 0), axis=0, keepdims=True) for c in chunks)
            blist[pl.ds(base + q, 1), :] = found

    index1 = lax.broadcasted_iota(I32, (1, BLK), 1)
    for v in range(NVAR):
        k = lax.shift_right_logical(index1, 6)
        d, b, g = roles(v, digits(index1 & 63))
        own = Y_TWO + ((b - 1) * 4 + g) * 8 + k
        loc = jnp.where(b > 0, own, jnp.where(g > 0, Y_ONE + (g - 1) * 8 + k, k))
        loc_c = column(loc)
        for o in range(4):
            block = jnp.where(d == 0, tabs[v * 4 + o], 64)
            key = block * 128 + lane1
            block_c, key_c = column(block), column(key)
            rank = jnp.sum(hits(key_c < key), axis=0, keepdims=True)
            begin = jnp.sum(hits(block_c < block), axis=0, keepdims=True)
            rank_c, begin_c = column(rank), column(begin)
            value = loc_c + o * 2 + 512 * hits(rank_c == begin_c)
            found = jnp.sum(jnp.where(rank_c == lane, value, 0), axis=0, keepdims=True)
            upto = jnp.sum(hits(block_c <= lane), axis=0, keepdims=True)
            count = jnp.sum(hits(block_c == lane), axis=0, keepdims=True)
            rlist[pl.ds((v * 4 + o) * 2, 1), :] = found
            rlist[pl.ds((v * 4 + o) * 2 + 1, 1), :] = jnp.where(count > 0, upto - 1, 32)

    to_sm = [
        pltpu.make_async_copy(a, b, sm_sem.at[1 + i])
        for i, (a, b) in enumerate(((flist, flist_sm), (blist, blist_sm), (ends, ends_sm), (rlist, rlist_sm)))
    ]
    for cp in to_sm:
        cp.start()

    for v in range(NVAR):
        for dc in (1, 3, 2, 0):
            await_arrival(x[v].at[pl.ds(X_HOP + (dc * 4 + 1) * 8, 24)], s2_r.at[v * 4 + dc])
            if dc:
                for b in (1, 3, 2):
                    pass_on(v, b, dc)
    runs[RUN_ZERO] = jnp.zeros((BLK, BLK), BF16)
    gt[0] = jnp.zeros((BLK, BLK), BF16)
    for cp in to_sm:
        cp.wait()
    for v in range(NVAR):
        await_arrival(x[v].at[pl.ds(X_END, 96)], s3_r.at[v])
    loads[2].wait()

    def forward_unit(u, acc):
        r, q = lax.div(u, 16), lax.rem(u, 16) * FC
        left, right = [], []
        for i in range(FC):
            left.append(w[flist_sm[r, q + i]])
            for v in range(NVAR):
                right.append(x[v][flist_sm[(v + 1) * 8 + r, q + i]])
        got = jnp.dot(
            jnp.concatenate(left, axis=1), jnp.concatenate(right, axis=0), preferred_element_type=F32
        )
        acc = jnp.where(flist_sm[32 + r, q] > 0, 0.0, acc) + got
        runs[u] = acc.astype(BF16)
        return acc

    lax.fori_loop(0, FU, forward_unit, jnp.zeros((BLK, BLK), F32), unroll=16)

    half = NB // 2
    mine, theirs = feat * half, (1 - feat) * half
    for i in range(half):
        send_a[i] = runs[ends_sm[2, theirs + i]]
    send(send_a, full.at[feat], feat_s.at[0], feat_r.at[0], other)
    for cp in loads[:2]:
        cp.wait()
    for i in range(half):
        full[feat, i] = runs[ends_sm[2, mine + i]]
    await_arrival(full.at[1 - feat], feat_r.at[0])

    wt[...] = jnp.zeros_like(wt)
    for i in range(half):
        left, right = full[0, i], full[1, i]
        pre = jnp.dot(left, weight[0:BLK, :], preferred_element_type=F32)
        pre += jnp.dot(right, weight[BLK:, :], preferred_element_type=F32)
        sig = jax.nn.sigmoid(pre)
        nodes = pl.ds(i * BLK, BLK)
        hidden[nodes, :] = (pre * sig).astype(BF16)
        grad = (cot[nodes, :].astype(F32) * (sig * (1.0 + pre * (1.0 - sig)))).astype(BF16)
        send_g[i] = lax.dot_general(
            weight[pl.ds((1 - feat) * BLK, BLK), :], grad, (((1,), (1,)), ((), ())), preferred_element_type=F32
        ).astype(BF16)
        send(send_g.at[i], gt.at[1 + mine + i], feat_s.at[1], feat_r.at[1], other)
        gt[1 + mine + i] = lax.dot_general(
            weight[pl.ds(feat * BLK, BLK), :], grad, (((1,), (1,)), ((), ())), preferred_element_type=F32
        ).astype(BF16)
        for h, part in ((0, left), (1, right)):
            wt[h] += lax.dot_general(part, grad, (((0,), (0,)), ((), ())), preferred_element_type=F32)
    send(wt.at[1 - feat], wt_in, feat_s.at[2], feat_r.at[2], other)
    hidden_cp = pltpu.make_async_copy(hidden, hidden_hbm, in_sem.at[0])
    hidden_cp.start()
    await_arrival(gt.at[pl.ds(1 + theirs, half)], feat_r.at[1])

    def backward_unit(u, acc):
        r, q = lax.div(u, 64), lax.rem(u, 64) * BC
        left = [gt[blist_sm[8 + r, q + i]] for i in range(BC)]
        right = [w[blist_sm[r, q + i]] for i in range(BC)]
        got = jnp.dot(
            jnp.concatenate(left, axis=1), jnp.concatenate(right, axis=0), preferred_element_type=F32
        )
        acc = jnp.where(blist_sm[16 + r, q] > 0, 0.0, acc) + got
        runs[u] = acc.astype(BF16)
        return acc

    lax.fori_loop(0, BU, backward_unit, jnp.zeros((BLK, BLK), F32), unroll=39)

    for v in range(NVAR):
        await_arrival(y[v].at[pl.ds(32, 96)], s2_s.at[v])

    def fill(v, g, b):
        for d in range(4):
            t = turn[v]
            z = lax.rem(cz + jnp.where(t == 0, d, jnp.where(t == 1, g, b)), 4)
            xx = lax.rem(cx + jnp.where(t == 0, b, jnp.where(t == 1, d, g)), 4)
            yy = lax.rem(cy + jnp.where(t == 0, g, jnp.where(t == 1, b, d)), 4)
            slot = NB + (z * 16 + xx * 4 + yy) * 2
            for k in range(2):
                s = slot + k
                run = ends_sm[lax.div(s, BLK), lax.rem(s, BLK)]
                y[v][(g * 4 + b) * 8 + d * 2 + k] = runs[run, pl.ds(FIRST[v], ROWS[v])]

    def go_back(v, lam, kap):
        src = y[v].at[pl.ds(lam * 8, 8)] if kap == 0 else y[v].at[pl.ds(Y_ONE + (lam * 3 + kap - 1) * 8, 8)]
        send(
            src, y[v].at[pl.ds(Y_TWO + ((4 - lam - 1) * 4 + kap) * 8, 8)],
            b2_s.at[v], b2_r.at[v], peer(v, 1, lam),
        )

    for b in (1, 3, 2, 0):
        for v in range(NVAR):
            for g in OFFS:
                fill(v, g, b)
                send(
                    y[v].at[pl.ds((g * 4 + b) * 8, 8)],
                    y[v].at[pl.ds(Y_ONE + (b * 3 + (4 - g - 1)) * 8, 8)],
                    b3_s.at[v], b3_r.at[v * 4 + b], peer(v, 2, g),
                )
            fill(v, 0, b)
            if b:
                go_back(v, b, 0)

    await_arrival(wt_in, feat_r.at[2])
    wt[feat] = wt[feat] + wt_in[...]

    def gw_copy(n, src, dst, axis, off):
        send(src, dst, gw_s.at[n], gw_r.at[n], (moved(axis == 0, axis == 1, off), feat))

    for off in OFFS:
        to = lax.rem(cz + off, 4)
        gw_copy(0, wt.at[feat, pl.ds(to * 32, 32)], gw0.at[off], 0, off)

    for b in (1, 3, 2):
        for v in range(NVAR):
            await_arrival(y[v].at[pl.ds(Y_ONE + b * 24, 24)], b3_r.at[v * 4 + b])
            for kap in (3, 1, 2):
                go_back(v, b, kap)
        if b == 1:
            await_arrival(gw0.at[pl.ds(1, 3)], gw_r.at[0])
            gw0[0] = wt[feat, pl.ds(cz * 32, 32)] + gw0[1] + gw0[2] + gw0[3]
            for off in OFFS:
                to = lax.rem(cx + off, 4)
                gw_copy(1, gw0.at[0, pl.ds(to * 8, 8)], gw1.at[off], 1, off)
        if b == 3:
            await_arrival(gw1.at[pl.ds(1, 3)], gw_r.at[1])
            gw2[cy] = gw0[0, pl.ds(cx * 8, 8)] + gw1[1] + gw1[2] + gw1[3]
            for off in OFFS:
                gw_copy(2, gw2.at[cy], gw2.at[cy], 2, off)
    await_arrival(gw1.at[pl.ds(1, 3)], gw_r.at[2])
    scale = float(64 * NB * BLK) ** (-0.5)
    gw3[cz, pl.ds(cx * 8, 8)] = (gw2[0] + gw2[1] + gw2[2] + gw2[3]) * scale
    for off in OFFS:
        gw_copy(3, gw3.at[cz, pl.ds(cx * 8, 8)], gw3.at[cz, pl.ds(cx * 8, 8)], 1, off)

    for v in range(NVAR):
        await_arrival(y[v].at[pl.ds(Y_ONE, 24)], b3_r.at[v * 4])
    for v in range(NVAR):
        n = ROWS[v]
        await_arrival(y[v].at[pl.ds(Y_TWO, 96)], b2_r.at[v])
        for o in (1, 3, 2, 0):
            r = (v * 4 + o) * 2

            def add(q, acc, v=v, r=r):
                code = rlist_sm[r, q]
                acc = jnp.where(code >= 512, 0.0, acc) + y[v][jnp.minimum(code & 511, Y_SIZE - 1)].astype(F32)
                rr[v][q] = acc.astype(BF16)
                return acc

            lax.fori_loop(0, 32, add, jnp.zeros((n, BLK), F32), unroll=4)
            rr[v][32] = jnp.zeros((n, BLK), BF16)
            for j in range(NB):
                ag[v][o * NB + j] = rr[v][rlist_sm[r + 1, j]]
            if o:
                send(
                    ag[v].at[pl.ds(o * NB, NB)], vin[v].at[pl.ds((4 - o - 1) * NB, NB)],
                    b1_s.at[v], b1_r.at[v], peer(v, 0, o),
                )

    await_arrival(gw1.at[pl.ds(1, 3)], gw_r.at[3])
    for off in OFFS:
        gw_copy(4, gw3.at[cz], gw3.at[cz], 0, off)

    for v in range(NVAR):
        await_arrival(vin[v], b1_r.at[v])
    for j in range(NB):
        run = ends_sm[0, j]
        parts = []
        for v in range(NVAR):
            total = runs[run, pl.ds(FIRST[v], ROWS[v])].astype(F32) + ag[v][j].astype(F32)
            for off in range(3):
                total += vin[v][off * NB + j].astype(F32)
            parts.append(total)
        grad_out[pl.ds(j * BLK, BLK), :] = jnp.transpose(jnp.concatenate(parts, axis=0)).astype(BF16)

    await_arrival(gw0.at[pl.ds(1, 3)], gw_r.at[4])
    for z in range(4):
        gw_out[pl.ds(z * 32, 32), :] = gw3[z]

    hidden_cp.wait()
    await_arrival(tabs.at[pl.ds(0, 9)], tab_s.at[0])
    await_arrival(send_a, feat_s.at[0])
    await_arrival(send_g, feat_s.at[1])
    await_arrival(wt_in, feat_s.at[2])
    for v in range(NVAR):
        await_arrival(ag[v].at[pl.ds(NB, 3 * NB)], s1_s.at[v])
        await_arrival(x[v].at[pl.ds(X_HOP + 32, 96)], s3_s.at[v])
        await_arrival(y[v].at[pl.ds(32, 96)], b3_s.at[v])
        await_arrival(y[v].at[pl.ds(Y_TWO, 96)], b2_s.at[v])
        await_arrival(ag[v].at[pl.ds(NB, 3 * NB)], b1_s.at[v])
    for n, ref in enumerate((gw0, gw1, gw1, gw1, gw0)):
        await_arrival(ref.at[pl.ds(1, 3)], gw_s.at[n])


def hand_over(*refs):
    n = (len(refs) - 1) // 3
    sem = refs[-1]
    inward = [pltpu.make_async_copy(refs[i], refs[2 * n + i], sem.at[i]) for i in range(n)]
    outward = [pltpu.make_async_copy(refs[2 * n + i], refs[n + i], sem.at[n + i]) for i in range(n)]
    for cp in inward:
        cp.start()
    for a, b in zip(inward, outward):
        a.wait()
        b.start()
    for cp in outward:
        cp.wait()


def local(features, tile_weights, tile_rows, tile_slots, send_blocks, weight, cotangent):
    dma = lambda n: pltpu.SemaphoreType.DMA((n,))
    vmem = lambda *shape, dtype=BF16: pltpu.VMEM(shape, dtype)
    smem = lambda *shape: pltpu.SMEM(shape, I32)
    in_vmem = pl.BlockSpec(memory_space=pltpu.VMEM)
    anywhere = pl.BlockSpec(memory_space=pl.ANY)
    nodes = NB * BLK
    scratch = [
        vmem(TILES, BLK, BLK),
        *[vmem(X_SIZE, n, BLK) for n in ROWS],
        *[vmem(Y_SIZE, n, BLK) for n in ROWS],
        *[vmem(4 * NB, n, BLK) for n in ROWS],
        *[vmem(3 * NB, n, BLK) for n in ROWS],
        *[vmem(33, n, BLK) for n in ROWS],
        vmem(BU + 1, BLK, BLK),
        vmem(12, 1, BLK, dtype=I32), smem(12, 1, BLK),
        vmem(40, BLK, dtype=I32), smem(40, BLK),
        vmem(24, BLK, dtype=I32), smem(24, BLK),
        vmem(8, BLK, dtype=I32), smem(8, BLK),
        vmem(24, BLK, dtype=I32), smem(24, BLK),
        vmem(256, 256), vmem(nodes // 2, 256), vmem(nodes // 2, 256), vmem(1, BLK, dtype=I32),
        vmem(2, NB // 2, BLK, BLK), vmem(NB // 2, BLK, BLK), vmem(NB + 1, BLK, BLK), vmem(NB // 2, BLK, BLK),
        vmem(2, BLK, 256, dtype=F32), vmem(BLK, 256, dtype=F32),
        vmem(4, 32, 256, dtype=F32), vmem(4, 8, 256, dtype=F32), vmem(4, 8, 256, dtype=F32),
        vmem(4, 32, 256, dtype=F32),
        dma(3), dma(5), dma(3), dma(3), dma(1), dma(1),
        dma(3), dma(3), dma(3), dma(12), dma(3), dma(3),
        dma(3), dma(12), dma(3), dma(3), dma(3), dma(3), dma(5), dma(5),
    ]
    out_shape = (
        jax.ShapeDtypeStruct((nodes // 2, 256), BF16),
        jax.ShapeDtypeStruct((nodes, BLK), BF16),
        jax.ShapeDtypeStruct((BLK, 256), F32),
    )
    results = pl.pallas_call(
        body,
        out_shape=out_shape,
        in_specs=[in_vmem, anywhere, in_vmem, in_vmem, in_vmem, anywhere, anywhere],
        out_specs=(anywhere, in_vmem, in_vmem),
        scratch_shapes=scratch,
        compiler_params=pltpu.CompilerParams(
            collective_id=0, has_side_effects=True, vmem_limit_bytes=64 * 2**20 - 2**16
        ),
        cost_estimate=pl.CostEstimate(flops=6 * 10**9, bytes_accessed=24 * 2**20, transcendentals=400000),
    )(
        features.reshape(NB, BLK, BLK), tile_weights, tile_rows.reshape(5, BLK), tile_slots.reshape(5, BLK),
        jnp.swapaxes(send_blocks, 1, 2).reshape(2, 64), weight, cotangent,
    )
    return pl.pallas_call(
        hand_over,
        out_shape=out_shape,
        in_specs=[anywhere] * 3,
        out_specs=(anywhere,) * 3,
        scratch_shapes=[*[pltpu.VMEM(o.shape, o.dtype) for o in out_shape], dma(6)],
    )(*results)


def solution(mesh):
    placed = (
        P("dom", "feat"),
        P("dom", None, None),
        P("dom"),
        P("dom"),
        P("dom", None, None),
        P(),
        P(("dom", "feat"), None),
    )
    return jax.shard_map(
        local,
        mesh=mesh,
        in_specs=placed,
        out_specs=(P(("dom", "feat"), None), P("dom", "feat"), P("feat", None)),
        check_vma=False,
    )
```

```python
import functools

import jax
import jax.numpy as jnp
from jax import lax
from jax.experimental import pallas as pl
from jax.experimental.pallas import tpu as pltpu
from jax.sharding import PartitionSpec as P

MESH = pl.DeviceIdType.MESH
F32, BF16, I32 = jnp.float32, jnp.bfloat16, jnp.int32

BLK = 128
NB = 12
TILES = 640
SIDE = 4
NVAR = 3
ROWS = (48, 48, 32)
FIRST = (0, 48, 96)

FC, BC = 8, 2
FU = 96
BU = 390
FCH, BCH = 6, 7

X_OWN, X_HOP, X_END, X_SIZE = 1, 16, 144, 240
Y_ONE, Y_TWO, Y_SIZE = 128, 224, 320
RUN_ZERO = BU
OFFS = (1, 3, 2)


def body(
    feats, tiles_hbm, rows_ref, slots_ref, tab_in, weight_hbm, cot_hbm,
    hidden_hbm, grad_out, gw_out,
    w, x0, x1, x2, y0, y1, y2, ag0, ag1, ag2, v0, v1, v2, rr0, rr1, rr2,
    runs, tabs, tabs_sm, own_sm, flist, flist_sm, blist, blist_sm, ends, ends_sm, rlist, rlist_sm,
    weight, cot, hidden, grads, tab_ref, full, send_a, gt, send_g, wt, wt_in, gw0, gw1, gw2, gw3,
    in_sem, sm_sem, feat_s, feat_r, tab_s, tab_r,
    s1_s, s1_r, s2_s, s2_r, s3_s, s3_r, b3_s, b3_r, b2_s, b2_r, b1_s, b1_r, gw_s, gw_r,
):
    x, y, ag, vin, rr = (x0, x1, x2), (y0, y1, y2), (ag0, ag1, ag2), (v0, v1, v2), (rr0, rr1, rr2)
    dom, feat = lax.axis_index("dom"), lax.axis_index("feat")
    cz, cx, cy = lax.div(dom, 16), lax.rem(lax.div(dom, 4), 4), lax.rem(dom, 4)

    def moved(axis_is_z, axis_is_x, off):
        z = lax.rem(cz + off, 4) * 16 + cx * 4 + cy
        xx = cz * 16 + lax.rem(cx + off, 4) * 4 + cy
        yy = cz * 16 + cx * 4 + lax.rem(cy + off, 4)
        return jnp.where(axis_is_z, z, jnp.where(axis_is_x, xx, yy))

    turn = [lax.rem(v + feat, 3) for v in range(NVAR)]

    def role(v, which):
        axis = lax.rem(turn[v] + which, 3)
        return axis == 0, axis == 1

    def peer(v, which, off):
        return (moved(*role(v, which), off), feat)

    def reader(v, db, dc):
        z, xx, yy = (lax.rem(c + d, 4) for c, d in ((cz, 0), (cx, 0), (cy, 0)))
        t = turn[v]
        z = lax.rem(cz + jnp.where(t == 1, dc, jnp.where(t == 2, db, 0)), 4)
        xx = lax.rem(cx + jnp.where(t == 0, db, jnp.where(t == 2, dc, 0)), 4)
        yy = lax.rem(cy + jnp.where(t == 0, dc, jnp.where(t == 1, db, 0)), 4)
        return z * 16 + xx * 4 + yy

    def send(src, dst, ssem, rsem, device):
        cp = pltpu.make_async_remote_copy(
            src_ref=src, dst_ref=dst, send_sem=ssem, recv_sem=rsem, device_id=device, device_id_type=MESH
        )
        cp.start()
        return cp

    def await_arrival(ref, sem):
        pltpu.make_async_copy(ref, ref, sem).wait()

    other = (dom, 1 - feat)

    barrier = pltpu.get_barrier_semaphore()
    for axis in range(3):
        for off in (1, 2, 3):
            pl.semaphore_signal(
                barrier, inc=1, device_id=(moved(axis == 0, axis == 1, off), feat), device_id_type=MESH
            )
    pl.semaphore_signal(barrier, inc=1, device_id=other, device_id_type=MESH)
    pl.semaphore_wait(barrier, 10)

    tab_ref[...] = jnp.concatenate([tab_in[0:1, :], tab_in[1:2, :]], axis=1)
    own_cp = pltpu.make_async_copy(tab_ref, own_sm, sm_sem.at[5])
    own_cp.start()
    for v in range(NVAR):
        for off in OFFS:
            send(tab_ref, tabs.at[v * 4 + (4 - off)], tab_s.at[0], tab_r.at[0], peer(v, 0, off))
    for off in OFFS:
        for v in range(NVAR):
            send(
                feats.at[:, pl.ds(FIRST[v], ROWS[v])], ag[v].at[pl.ds((4 - off) * NB, NB)],
                s1_s.at[v], s1_r.at[v], peer(v, 0, off),
            )
    loads = [
        pltpu.make_async_copy(a, b, in_sem.at[i])
        for i, (a, b) in enumerate(((weight_hbm, weight), (cot_hbm, cot), (tiles_hbm, w)))
    ]
    for cp in loads:
        cp.start()

    for v in range(NVAR):
        chunk = pl.ds(FIRST[v], ROWS[v])
        x[v][0] = jnp.zeros((ROWS[v], BLK), BF16)
        for j in range(NB):
            block = feats[j, chunk]
            x[v][X_OWN + j] = block
            ag[v][j] = block
        tabs[v * 4] = tab_ref[...]

    def hop(v, db, dc, begin, n):
        send(
            y[v].at[pl.ds((db * 4 + dc) * 8 + begin, n)],
            x[v].at[pl.ds(X_HOP + (dc * 4 + (4 - db)) * 8 + begin, n)],
            s2_s.at[v], s2_r.at[v * 4 + dc], peer(v, 1, db),
        )

    own_cp.wait()
    for v in range(NVAR):
        for dc in (1, 3, 2, 0):
            for db in OFFS:
                at = reader(v, db, dc)
                for k in range(2):
                    y[v][(db * 4 + dc) * 8 + k] = feats[own_sm[0, at + k * 64], pl.ds(FIRST[v], ROWS[v])]
                hop(v, db, dc, 0, 2)

    lane = lax.broadcasted_iota(I32, (BLK, BLK), 1)
    sub = lax.broadcasted_iota(I32, (BLK, BLK), 0)
    ones = jnp.ones((BLK, BLK), I32)

    def column(row):
        return jnp.transpose(ones * row)

    def hits(mask):
        return jnp.where(mask, 1, 0)

    chunks = range(TILES // BLK)

    row_r = [rows_ref[pl.ds(c, 1), :] for c in chunks]
    slot_r = [slots_ref[pl.ds(c, 1), :] for c in chunks]
    row_c = [column(r) for r in row_r]
    lane1 = lane[0:1]
    row_count = sum(jnp.sum(hits(r == lane), axis=0, keepdims=True) for r in row_c)
    row_units = lax.shift_right_logical(row_count + (FC - 1), FC.bit_length() - 1)
    row_units_c, row_count_c = column(row_units), column(row_count)
    row_first = jnp.sum(jnp.where(sub < lane, row_units_c, 0), axis=0, keepdims=True)
    row_begin = jnp.sum(jnp.where(sub < lane, row_count_c, 0), axis=0, keepdims=True)
    row_last = jnp.where(row_count > 0, row_first + row_units - 1, RUN_ZERO)
    ends[pl.ds(2, 1), :] = row_last

    def digits(block):
        pz, px, py = lax.shift_right_logical(block, 4), lax.shift_right_logical(block, 2) & 3, block & 3
        return (pz - cz) & 3, (px - cx) & 3, (py - cy) & 3

    def roles(v, rel):
        rz, rx, ry = rel
        t = turn[v]
        first = jnp.where(t == 0, rz, jnp.where(t == 1, rx, ry))
        second = jnp.where(t == 0, rx, jnp.where(t == 1, ry, rz))
        third = jnp.where(t == 0, ry, jnp.where(t == 1, rz, rx))
        return first, second, third

    def x_entry(v, slot):
        far = jnp.maximum(slot - NB, 0)
        k = far & 1
        d, b, g = roles(v, digits(lax.shift_right_logical(far, 1)))
        near = X_HOP + b * 8 + d * 2 + k
        end = X_END + (((g - 1) * 4 + b) * 4 + d) * 2 + k
        return jnp.where(slot < NB, X_OWN + slot, jnp.where(g == 0, near, end))

    place, tile_c = [], []
    for c in chunks:
        offset = jnp.sum(jnp.where(row_c[c] == lane, FC * row_first - row_begin, 0), axis=1, keepdims=True)
        tile_c.append(sub + c * BLK)
        place.append(offset + tile_c[c])
    for v in range(NVAR):
        entry_c = [column(x_entry(v, s)) for s in slot_r]
        for q in range(FCH):
            at = lane + q * BLK
            found = sum(
                jnp.sum(jnp.where(place[c] == at, entry_c[c], 0), axis=0, keepdims=True) for c in chunks
            )
            flist[pl.ds((v + 1) * 8 + q, 1), :] = found
    for q in range(FCH):
        at = lane + q * BLK
        found = sum(
            jnp.sum(jnp.where(place[c] == at, tile_c[c], 0), axis=0, keepdims=True) for c in chunks
        )
        flist[pl.ds(q, 1), :] = found
        starts = sum(
            jnp.sum(
                jnp.where(
                    (place[c] == at)
                    & (tile_c[c] == jnp.sum(jnp.where(row_c[c] == lane, row_begin, 0), axis=1, keepdims=True)),
                    1, 0,
                ),
                axis=0, keepdims=True,
            )
            for c in chunks
        )
        flist[pl.ds(32 + q, 1), :] = starts

    await_arrival(tabs.at[pl.ds(0, 9)], tab_r.at[0])
    tabs_cp = pltpu.make_async_copy(tabs, tabs_sm, sm_sem.at[0])
    tabs_cp.start()
    tabs_cp.wait()

    def pack(v, db, dc, dst, base):
        at = reader(v, db, dc)
        for d in range(1 if db else 0, 4):
            for k in range(2):
                j = tabs_sm[v * 4 + d, 0, at + k * 64]
                dst[base + d * 2 + k] = ag[v][d * NB + j]

    def pass_on(v, b, dc):
        send(
            x[v].at[pl.ds(X_HOP + (dc * 4 + b) * 8, 8)],
            x[v].at[pl.ds(X_END + ((4 - dc - 1) * 4 + b) * 8, 8)],
            s3_s.at[v], s3_r.at[v], peer(v, 2, dc),
        )

    for v in range(NVAR):
        await_arrival(ag[v].at[pl.ds(NB, 3 * NB)], s1_r.at[v])
        for dc in (1, 3, 2, 0):
            pack(v, 0, dc, x[v], X_HOP + dc * 32)
            if dc:
                pass_on(v, 0, dc)
            for db in OFFS:
                base = (db * 4 + dc) * 8
                pack(v, db, dc, y[v], base)
                hop(v, db, dc, 2, 6)

    slot_c = [column(s) for s in slot_r]
    counts = [sum(jnp.sum(hits(s == lane + h * BLK), axis=0, keepdims=True) for s in slot_c) for h in range(2)]
    units = [lax.shift_right_logical(n + (BC - 1), BC.bit_length() - 1) for n in counts]
    units_c = [column(u) for u in units]
    firsts = [
        jnp.sum(jnp.where(sub < lane, units_c[0], 0), axis=0, keepdims=True),
        jnp.sum(jnp.where(sub < lane, units_c[1], 0) + units_c[0], axis=0, keepdims=True),
    ]
    for h in range(2):
        last = jnp.where(counts[h] > 0, firsts[h] + units[h] - 1, RUN_ZERO)
        ends[pl.ds(h, 1), :] = last
    order, place = [], []
    for c in chunks:
        before = sum(hits((slot_c[c] == slot_r[e]) & (lane + e * BLK < tile_c[c])) for e in chunks)
        order.append(jnp.sum(before, axis=1, keepdims=True))
        begin = jnp.sum(
            sum(jnp.where(slot_c[c] == lane + h * BLK, firsts[h], 0) for h in range(2)),
            axis=1, keepdims=True,
        )
        place.append(ones * (BC * begin + order[c]))
    start_c = [hits(o == 0) * ones for o in order]
    row_next = [r + 1 for r in row_c]
    for q in range(BCH):
        at = lane + q * BLK
        for base, what in ((0, tile_c), (8, row_next), (16, start_c)):
            found = sum(jnp.sum(jnp.where(place[c] == at, what[c], 0), axis=0, keepdims=True) for c in chunks)
            blist[pl.ds(base + q, 1), :] = found

    index1 = lax.broadcasted_iota(I32, (1, BLK), 1)
    for v in range(NVAR):
        k = lax.shift_right_logical(index1, 6)
        d, b, g = roles(v, digits(index1 & 63))
        own = Y_TWO + ((b - 1) * 4 + g) * 8 + k
        loc = jnp.where(b > 0, own, jnp.where(g > 0, Y_ONE + (g - 1) * 8 + k, k))
        loc_c = column(loc)
        for o in range(4):
            block = jnp.where(d == 0, tabs[v * 4 + o], 64)
            key = block * 128 + lane1
            block_c, key_c = column(block), column(key)
            rank = jnp.sum(hits(key_c < key), axis=0, keepdims=True)
            begin = jnp.sum(hits(block_c < block), axis=0, keepdims=True)
            rank_c, begin_c = column(rank), column(begin)
            value = loc_c + o * 2 + 512 * hits(rank_c == begin_c)
            found = jnp.sum(jnp.where(rank_c == lane, value, 0), axis=0, keepdims=True)
            upto = jnp.sum(hits(block_c <= lane), axis=0, keepdims=True)
            count = jnp.sum(hits(block_c == lane), axis=0, keepdims=True)
            rlist[pl.ds((v * 4 + o) * 2, 1), :] = found
            rlist[pl.ds((v * 4 + o) * 2 + 1, 1), :] = jnp.where(count > 0, upto - 1, 32)

    to_sm = [
        pltpu.make_async_copy(a, b, sm_sem.at[1 + i])
        for i, (a, b) in enumerate(((flist, flist_sm), (blist, blist_sm), (ends, ends_sm), (rlist, rlist_sm)))
    ]
    for cp in to_sm:
        cp.start()

    for v in range(NVAR):
        for dc in OFFS:
            await_arrival(x[v].at[pl.ds(X_HOP + (dc * 4 + 1) * 8, 24)], s2_r.at[v * 4 + dc])
            for b in (1, 3, 2):
                pass_on(v, b, dc)
    runs[RUN_ZERO] = jnp.zeros((BLK, BLK), BF16)
    gt[0] = jnp.zeros((BLK, BLK), BF16)
    for cp in to_sm:
        cp.wait()
    for v in range(NVAR):
        await_arrival(x[v].at[pl.ds(X_HOP + 8, 24)], s2_r.at[v * 4])
        await_arrival(x[v].at[pl.ds(X_END, 96)], s3_r.at[v])
    loads[2].wait()

    def forward_unit(u, acc):
        r, q = lax.div(u, 16), lax.rem(u, 16) * FC
        left, right = [], []
        for i in range(FC):
            left.append(w[flist_sm[r, q + i]])
            for v in range(NVAR):
                right.append(x[v][flist_sm[(v + 1) * 8 + r, q + i]])
        got = jnp.dot(
            jnp.concatenate(left, axis=1), jnp.concatenate(right, axis=0), preferred_element_type=F32
        )
        acc = jnp.where(flist_sm[32 + r, q] > 0, 0.0, acc) + got
        runs[u] = acc.astype(BF16)
        return acc

    lax.fori_loop(0, FU, forward_unit, jnp.zeros((BLK, BLK), F32), unroll=16)

    half, nodes_here = NB // 2, NB // 2 * BLK
    mine, theirs = feat * half, (1 - feat) * half
    for i in range(half):
        send_a[i] = runs[ends_sm[2, theirs + i]]
    send(send_a, full.at[feat], feat_s.at[0], feat_r.at[0], other)
    for cp in loads[:2]:
        cp.wait()
    for i in range(half):
        full[feat, i] = runs[ends_sm[2, mine + i]]
    await_arrival(full.at[1 - feat], feat_r.at[0])

    for i in range(half):
        left, right = full[0, i], full[1, i]
        pre = jnp.dot(left, weight[0:BLK, :], preferred_element_type=F32)
        pre += jnp.dot(right, weight[BLK:, :], preferred_element_type=F32)
        sig = jax.nn.sigmoid(pre)
        nodes = pl.ds(i * BLK, BLK)
        hidden[nodes, :] = (pre * sig).astype(BF16)
        grad = (cot[nodes, :].astype(F32) * (sig * (1.0 + pre * (1.0 - sig)))).astype(BF16)
        grads[nodes, :] = grad
        send_g[i] = lax.dot_general(
            weight[pl.ds((1 - feat) * BLK, BLK), :], grad, (((1,), (1,)), ((), ())), preferred_element_type=F32
        ).astype(BF16)
        send(send_g.at[i], gt.at[1 + mine + i], feat_s.at[1], feat_r.at[1], other)
        gt[1 + mine + i] = lax.dot_general(
            weight[pl.ds(feat * BLK, BLK), :], grad, (((1,), (1,)), ((), ())), preferred_element_type=F32
        ).astype(BF16)
    hidden_cp = pltpu.make_async_copy(hidden, hidden_hbm, in_sem.at[0])
    hidden_cp.start()
    await_arrival(gt.at[pl.ds(1 + theirs, half)], feat_r.at[1])

    def backward_unit(u, acc):
        r, q = lax.div(u, 64), lax.rem(u, 64) * BC
        left = [gt[blist_sm[8 + r, q + i]] for i in range(BC)]
        right = [w[blist_sm[r, q + i]] for i in range(BC)]
        got = jnp.dot(
            jnp.concatenate(left, axis=1), jnp.concatenate(right, axis=0), preferred_element_type=F32
        )
        acc = jnp.where(blist_sm[16 + r, q] > 0, 0.0, acc) + got
        runs[u] = acc.astype(BF16)
        return acc

    lax.fori_loop(0, BU, backward_unit, jnp.zeros((BLK, BLK), F32), unroll=39)

    for v in range(NVAR):
        await_arrival(y[v].at[pl.ds(32, 96)], s2_s.at[v])

    def fill(v, g, b):
        for d in range(4):
            t = turn[v]
            z = lax.rem(cz + jnp.where(t == 0, d, jnp.where(t == 1, g, b)), 4)
            xx = lax.rem(cx + jnp.where(t == 0, b, jnp.where(t == 1, d, g)), 4)
            yy = lax.rem(cy + jnp.where(t == 0, g, jnp.where(t == 1, b, d)), 4)
            slot = NB + (z * 16 + xx * 4 + yy) * 2
            for k in range(2):
                s = slot + k
                run = ends_sm[lax.div(s, BLK), lax.rem(s, BLK)]
                y[v][(g * 4 + b) * 8 + d * 2 + k] = runs[run, pl.ds(FIRST[v], ROWS[v])]

    def go_back(v, lam, kap):
        src = y[v].at[pl.ds(lam * 8, 8)] if kap == 0 else y[v].at[pl.ds(Y_ONE + (lam * 3 + kap - 1) * 8, 8)]
        send(
            src, y[v].at[pl.ds(Y_TWO + ((4 - lam - 1) * 4 + kap) * 8, 8)],
            b2_s.at[v], b2_r.at[v], peer(v, 1, lam),
        )

    for v in range(NVAR):
        for b in (1, 3, 2, 0):
            for g in OFFS:
                fill(v, g, b)
                send(
                    y[v].at[pl.ds((g * 4 + b) * 8, 8)],
                    y[v].at[pl.ds(Y_ONE + (b * 3 + (4 - g - 1)) * 8, 8)],
                    b3_s.at[v], b3_r.at[v * 4 + b], peer(v, 2, g),
                )
            fill(v, 0, b)
            if b:
                go_back(v, b, 0)

    for h in range(2):
        part = full[h].reshape(nodes_here, BLK)
        wt[h] = lax.dot_general(part, grads[...], (((0,), (0,)), ((), ())), preferred_element_type=F32)
    send(wt.at[1 - feat], wt_in, feat_s.at[2], feat_r.at[2], other)

    def gw_copy(n, src, dst, axis, off):
        send(src, dst, gw_s.at[n], gw_r.at[n], (moved(axis == 0, axis == 1, off), feat))

    def gw_step(n):
        if n == 0:
            await_arrival(wt_in, feat_r.at[2])
            wt[feat] = wt[feat] + wt_in[...]
            for off in OFFS:
                gw_copy(0, wt.at[feat, pl.ds(lax.rem(cz + off, 4) * 32, 32)], gw0.at[off], 0, off)
        elif n == 1:
            await_arrival(gw0.at[pl.ds(1, 3)], gw_r.at[0])
            gw0[0] = wt[feat, pl.ds(cz * 32, 32)] + gw0[1] + gw0[2] + gw0[3]
            for off in OFFS:
                gw_copy(1, gw0.at[0, pl.ds(lax.rem(cx + off, 4) * 8, 8)], gw1.at[off], 1, off)
        elif n == 2:
            await_arrival(gw1.at[pl.ds(1, 3)], gw_r.at[1])
            gw2[cy] = gw0[0, pl.ds(cx * 8, 8)] + gw1[1] + gw1[2] + gw1[3]
            for off in OFFS:
                gw_copy(2, gw2.at[cy], gw2.at[cy], 2, off)
        elif n == 3:
            await_arrival(gw1.at[pl.ds(1, 3)], gw_r.at[2])
            scale = float(64 * NB * BLK) ** (-0.5)
            gw3[cz, pl.ds(cx * 8, 8)] = (gw2[0] + gw2[1] + gw2[2] + gw2[3]) * scale
            for off in OFFS:
                gw_copy(3, gw3.at[cz, pl.ds(cx * 8, 8)], gw3.at[cz, pl.ds(cx * 8, 8)], 1, off)
        else:
            await_arrival(gw1.at[pl.ds(1, 3)], gw_r.at[3])
            for off in OFFS:
                gw_copy(4, gw3.at[cz], gw3.at[cz], 0, off)

    for v in range(NVAR):
        for b in (1, 3, 2):
            await_arrival(y[v].at[pl.ds(Y_ONE + b * 24, 24)], b3_r.at[v * 4 + b])
            for kap in (3, 1, 2):
                go_back(v, b, kap)
        gw_step(v)

    for v in range(NVAR):
        n = ROWS[v]
        await_arrival(y[v].at[pl.ds(Y_ONE, 24)], b3_r.at[v * 4])
        await_arrival(y[v].at[pl.ds(Y_TWO, 96)], b2_r.at[v])
        for o in (1, 3, 2, 0):
            r = (v * 4 + o) * 2

            def add(q, acc, v=v, r=r):
                code = rlist_sm[r, q]
                acc = jnp.where(code >= 512, 0.0, acc) + y[v][jnp.minimum(code & 511, Y_SIZE - 1)].astype(F32)
                rr[v][q] = acc.astype(BF16)
                return acc

            lax.fori_loop(0, 32, add, jnp.zeros((n, BLK), F32), unroll=4)
            rr[v][32] = jnp.zeros((n, BLK), BF16)
            for j in range(NB):
                ag[v][o * NB + j] = rr[v][rlist_sm[r + 1, j]]
            if o:
                send(
                    ag[v].at[pl.ds(o * NB, NB)], vin[v].at[pl.ds((4 - o - 1) * NB, NB)],
                    b1_s.at[v], b1_r.at[v], peer(v, 0, o),
                )
        if v < 2:
            gw_step(3 + v)

    for v in range(NVAR):
        await_arrival(vin[v], b1_r.at[v])
    for j in range(NB):
        run = ends_sm[0, j]
        parts = []
        for v in range(NVAR):
            total = runs[run, pl.ds(FIRST[v], ROWS[v])].astype(F32) + ag[v][j].astype(F32)
            for off in range(3):
                total += vin[v][off * NB + j].astype(F32)
            parts.append(total)
        grad_out[pl.ds(j * BLK, BLK), :] = jnp.transpose(jnp.concatenate(parts, axis=0)).astype(BF16)

    await_arrival(gw0.at[pl.ds(1, 3)], gw_r.at[4])
    for z in range(4):
        gw_out[pl.ds(z * 32, 32), :] = gw3[z]

    hidden_cp.wait()
    await_arrival(tabs.at[pl.ds(0, 9)], tab_s.at[0])
    await_arrival(send_a, feat_s.at[0])
    await_arrival(send_g, feat_s.at[1])
    await_arrival(wt_in, feat_s.at[2])
    for v in range(NVAR):
        await_arrival(ag[v].at[pl.ds(NB, 3 * NB)], s1_s.at[v])
        await_arrival(x[v].at[pl.ds(X_HOP + 32, 96)], s3_s.at[v])
        await_arrival(y[v].at[pl.ds(32, 96)], b3_s.at[v])
        await_arrival(y[v].at[pl.ds(Y_TWO, 96)], b2_s.at[v])
        await_arrival(ag[v].at[pl.ds(NB, 3 * NB)], b1_s.at[v])
    for n, ref in enumerate((gw0, gw1, gw1, gw1, gw0)):
        await_arrival(ref.at[pl.ds(1, 3)], gw_s.at[n])


def hand_over(*refs):
    n = (len(refs) - 1) // 3
    sem = refs[-1]
    inward = [pltpu.make_async_copy(refs[i], refs[2 * n + i], sem.at[i]) for i in range(n)]
    outward = [pltpu.make_async_copy(refs[2 * n + i], refs[n + i], sem.at[n + i]) for i in range(n)]
    for cp in inward:
        cp.start()
    for a, b in zip(inward, outward):
        a.wait()
        b.start()
    for cp in outward:
        cp.wait()


def local(features, tile_weights, tile_rows, tile_slots, send_blocks, weight, cotangent):
    dma = lambda n: pltpu.SemaphoreType.DMA((n,))
    vmem = lambda *shape, dtype=BF16: pltpu.VMEM(shape, dtype)
    smem = lambda *shape: pltpu.SMEM(shape, I32)
    in_vmem = pl.BlockSpec(memory_space=pltpu.VMEM)
    anywhere = pl.BlockSpec(memory_space=pl.ANY)
    nodes = NB * BLK
    scratch = [
        vmem(TILES, BLK, BLK),
        *[vmem(X_SIZE, n, BLK) for n in ROWS],
        *[vmem(Y_SIZE, n, BLK) for n in ROWS],
        *[vmem(4 * NB, n, BLK) for n in ROWS],
        *[vmem(3 * NB, n, BLK) for n in ROWS],
        *[vmem(33, n, BLK) for n in ROWS],
        vmem(BU + 1, BLK, BLK),
        vmem(12, 1, BLK, dtype=I32), smem(12, 1, BLK), smem(1, BLK),
        vmem(40, BLK, dtype=I32), smem(40, BLK),
        vmem(24, BLK, dtype=I32), smem(24, BLK),
        vmem(8, BLK, dtype=I32), smem(8, BLK),
        vmem(24, BLK, dtype=I32), smem(24, BLK),
        vmem(256, 256), vmem(nodes // 2, 256), vmem(nodes // 2, 256), vmem(nodes // 2, 256), vmem(1, BLK, dtype=I32),
        vmem(2, NB // 2, BLK, BLK), vmem(NB // 2, BLK, BLK), vmem(NB + 1, BLK, BLK), vmem(NB // 2, BLK, BLK),
        vmem(2, BLK, 256, dtype=F32), vmem(BLK, 256, dtype=F32),
        vmem(4, 32, 256, dtype=F32), vmem(4, 8, 256, dtype=F32), vmem(4, 8, 256, dtype=F32),
        vmem(4, 32, 256, dtype=F32),
        dma(3), dma(6), dma(3), dma(3), dma(1), dma(1),
        dma(3), dma(3), dma(3), dma(12), dma(3), dma(3),
        dma(3), dma(12), dma(3), dma(3), dma(3), dma(3), dma(5), dma(5),
    ]
    out_shape = (
        jax.ShapeDtypeStruct((nodes // 2, 256), BF16),
        jax.ShapeDtypeStruct((nodes, BLK), BF16),
        jax.ShapeDtypeStruct((BLK, 256), F32),
    )
    results = pl.pallas_call(
        body,
        out_shape=out_shape,
        in_specs=[in_vmem, anywhere, in_vmem, in_vmem, in_vmem, anywhere, anywhere],
        out_specs=(anywhere, in_vmem, in_vmem),
        scratch_shapes=scratch,
        compiler_params=pltpu.CompilerParams(
            collective_id=0, has_side_effects=True, vmem_limit_bytes=64 * 2**20 - 2**16
        ),
        cost_estimate=pl.CostEstimate(flops=6 * 10**9, bytes_accessed=24 * 2**20, transcendentals=400000),
    )(
        features.reshape(NB, BLK, BLK), tile_weights, tile_rows.reshape(5, BLK), tile_slots.reshape(5, BLK),
        jnp.swapaxes(send_blocks, 1, 2).reshape(2, 64), weight, cotangent,
    )
    return pl.pallas_call(
        hand_over,
        out_shape=out_shape,
        in_specs=[anywhere] * 3,
        out_specs=(anywhere,) * 3,
        scratch_shapes=[*[pltpu.VMEM(o.shape, o.dtype) for o in out_shape], dma(6)],
    )(*results)


def solution(mesh):
    placed = (
        P("dom", "feat"),
        P("dom", None, None),
        P("dom"),
        P("dom"),
        P("dom", None, None),
        P(),
        P(("dom", "feat"), None),
    )
    return jax.shard_map(
        local,
        mesh=mesh,
        in_specs=placed,
        out_specs=(P(("dom", "feat"), None), P("dom", "feat"), P("feat", None)),
        check_vma=False,
    )
```

```python
import functools

import jax
import jax.numpy as jnp
from jax import lax
from jax.experimental import pallas as pl
from jax.experimental.pallas import tpu as pltpu
from jax.sharding import PartitionSpec as P

MESH = pl.DeviceIdType.MESH
F32, BF16, I32 = jnp.float32, jnp.bfloat16, jnp.int32

BLK = 128
NB = 12
TILES = 640
SIDE = 4
NVAR = 3
ROWS = (48, 48, 32)
FIRST = (0, 48, 96)

FC, BC = 8, 2
FU = 96
BU = 390
FCH, BCH = 6, 7

X_OWN, X_HOP, X_END, X_SIZE = 1, 16, 144, 240
Y_ONE, Y_TWO, Y_SIZE = 128, 224, 320
RUN_ZERO = BU
OFFS = (1, 3, 2)


def body(
    feats_hbm, tiles_hbm, rows_hbm, slots_hbm, tab_hbm, weight_hbm, cot_hbm,
    hidden_hbm, grad_out, gw_out,
    w, x0, x1, x2, y0, y1, y2, ag0, ag1, ag2, v0, v1, v2, rr0, rr1, rr2,
    runs, tabs, tabs_sm, own_sm, flist, flist_sm, blist, blist_sm, ends, ends_sm, rlist, rlist_sm,
    weight, cot, hidden, grads, feats, rows_ref, slots_ref, tab_in, tab_ref, full, send_a, gt, send_g, wt, wt_in, gw0, gw1, gw2, gw3,
    in_sem, sm_sem, feat_s, feat_r, tab_s, tab_r,
    s1_s, s1_r, s2_s, s2_r, s3_s, s3_r, b3_s, b3_r, b2_s, b2_r, b1_s, b1_r, gw_s, gw_r,
):
    x, y, ag, vin, rr = (x0, x1, x2), (y0, y1, y2), (ag0, ag1, ag2), (v0, v1, v2), (rr0, rr1, rr2)
    dom, feat = lax.axis_index("dom"), lax.axis_index("feat")
    cz, cx, cy = lax.div(dom, 16), lax.rem(lax.div(dom, 4), 4), lax.rem(dom, 4)

    def moved(axis_is_z, axis_is_x, off):
        z = lax.rem(cz + off, 4) * 16 + cx * 4 + cy
        xx = cz * 16 + lax.rem(cx + off, 4) * 4 + cy
        yy = cz * 16 + cx * 4 + lax.rem(cy + off, 4)
        return jnp.where(axis_is_z, z, jnp.where(axis_is_x, xx, yy))

    turn = [lax.rem(v + feat, 3) for v in range(NVAR)]

    def role(v, which):
        axis = lax.rem(turn[v] + which, 3)
        return axis == 0, axis == 1

    def peer(v, which, off):
        return (moved(*role(v, which), off), feat)

    def reader(v, db, dc):
        z, xx, yy = (lax.rem(c + d, 4) for c, d in ((cz, 0), (cx, 0), (cy, 0)))
        t = turn[v]
        z = lax.rem(cz + jnp.where(t == 1, dc, jnp.where(t == 2, db, 0)), 4)
        xx = lax.rem(cx + jnp.where(t == 0, db, jnp.where(t == 2, dc, 0)), 4)
        yy = lax.rem(cy + jnp.where(t == 0, dc, jnp.where(t == 1, db, 0)), 4)
        return z * 16 + xx * 4 + yy

    def send(src, dst, ssem, rsem, device):
        cp = pltpu.make_async_remote_copy(
            src_ref=src, dst_ref=dst, send_sem=ssem, recv_sem=rsem, device_id=device, device_id_type=MESH
        )
        cp.start()
        return cp

    def await_arrival(ref, sem):
        pltpu.make_async_copy(ref, ref, sem).wait()

    other = (dom, 1 - feat)

    barrier = pltpu.get_barrier_semaphore()
    for axis in range(3):
        for off in (1, 2, 3):
            pl.semaphore_signal(
                barrier, inc=1, device_id=(moved(axis == 0, axis == 1, off), feat), device_id_type=MESH
            )
    pl.semaphore_signal(barrier, inc=1, device_id=other, device_id_type=MESH)
    first = [
        pltpu.make_async_copy(a, b, in_sem.at[3 + i])
        for i, (a, b) in enumerate(
            ((tab_hbm, tab_in), (feats_hbm, feats), (rows_hbm, rows_ref), (slots_hbm, slots_ref))
        )
    ]
    for cp in first:
        cp.start()
    for cp in first:
        cp.wait()
    pl.semaphore_wait(barrier, 10)

    tab_ref[...] = jnp.concatenate([tab_in[0:1, :], tab_in[1:2, :]], axis=1)
    own_cp = pltpu.make_async_copy(tab_ref, own_sm, sm_sem.at[5])
    own_cp.start()
    for v in range(NVAR):
        for off in OFFS:
            send(tab_ref, tabs.at[v * 4 + (4 - off)], tab_s.at[0], tab_r.at[0], peer(v, 0, off))
    for off in OFFS:
        for v in range(NVAR):
            send(
                feats.at[:, pl.ds(FIRST[v], ROWS[v])], ag[v].at[pl.ds((4 - off) * NB, NB)],
                s1_s.at[v], s1_r.at[v], peer(v, 0, off),
            )
    loads = [
        pltpu.make_async_copy(a, b, in_sem.at[i])
        for i, (a, b) in enumerate(((weight_hbm, weight), (cot_hbm, cot), (tiles_hbm, w)))
    ]
    for cp in loads:
        cp.start()

    for v in range(NVAR):
        chunk = pl.ds(FIRST[v], ROWS[v])
        x[v][0] = jnp.zeros((ROWS[v], BLK), BF16)
        for j in range(NB):
            block = feats[j, chunk]
            x[v][X_OWN + j] = block
            ag[v][j] = block
        tabs[v * 4] = tab_ref[...]

    def hop(v, db, dc, begin, n):
        send(
            y[v].at[pl.ds((db * 4 + dc) * 8 + begin, n)],
            x[v].at[pl.ds(X_HOP + (dc * 4 + (4 - db)) * 8 + begin, n)],
            s2_s.at[v], s2_r.at[v * 4 + dc], peer(v, 1, db),
        )

    own_cp.wait()
    for v in range(NVAR):
        for dc in (1, 3, 2, 0):
            for db in OFFS:
                at = reader(v, db, dc)
                for k in range(2):
                    y[v][(db * 4 + dc) * 8 + k] = feats[own_sm[0, at + k * 64], pl.ds(FIRST[v], ROWS[v])]
                hop(v, db, dc, 0, 2)

    lane = lax.broadcasted_iota(I32, (BLK, BLK), 1)
    sub = lax.broadcasted_iota(I32, (BLK, BLK), 0)
    ones = jnp.ones((BLK, BLK), I32)

    def column(row):
        return jnp.transpose(ones * row)

    def hits(mask):
        return jnp.where(mask, 1, 0)

    chunks = range(TILES // BLK)

    row_r = [rows_ref[pl.ds(c, 1), :] for c in chunks]
    slot_r = [slots_ref[pl.ds(c, 1), :] for c in chunks]
    row_c = [column(r) for r in row_r]
    lane1 = lane[0:1]
    row_count = sum(jnp.sum(hits(r == lane), axis=0, keepdims=True) for r in row_c)
    row_units = lax.shift_right_logical(row_count + (FC - 1), FC.bit_length() - 1)
    row_units_c, row_count_c = column(row_units), column(row_count)
    row_first = jnp.sum(jnp.where(sub < lane, row_units_c, 0), axis=0, keepdims=True)
    row_begin = jnp.sum(jnp.where(sub < lane, row_count_c, 0), axis=0, keepdims=True)
    row_last = jnp.where(row_count > 0, row_first + row_units - 1, RUN_ZERO)
    ends[pl.ds(2, 1), :] = row_last

    def digits(block):
        pz, px, py = lax.shift_right_logical(block, 4), lax.shift_right_logical(block, 2) & 3, block & 3
        return (pz - cz) & 3, (px - cx) & 3, (py - cy) & 3

    def roles(v, rel):
        rz, rx, ry = rel
        t = turn[v]
        first = jnp.where(t == 0, rz, jnp.where(t == 1, rx, ry))
        second = jnp.where(t == 0, rx, jnp.where(t == 1, ry, rz))
        third = jnp.where(t == 0, ry, jnp.where(t == 1, rz, rx))
        return first, second, third

    def x_entry(v, slot):
        far = jnp.maximum(slot - NB, 0)
        k = far & 1
        d, b, g = roles(v, digits(lax.shift_right_logical(far, 1)))
        near = X_HOP + b * 8 + d * 2 + k
        end = X_END + (((g - 1) * 4 + b) * 4 + d) * 2 + k
        return jnp.where(slot < NB, X_OWN + slot, jnp.where(g == 0, near, end))

    place, tile_c = [], []
    for c in chunks:
        offset = jnp.sum(jnp.where(row_c[c] == lane, FC * row_first - row_begin, 0), axis=1, keepdims=True)
        tile_c.append(sub + c * BLK)
        place.append(offset + tile_c[c])
    for v in range(NVAR):
        entry_c = [column(x_entry(v, s)) for s in slot_r]
        for q in range(FCH):
            at = lane + q * BLK
            found = sum(
                jnp.sum(jnp.where(place[c] == at, entry_c[c], 0), axis=0, keepdims=True) for c in chunks
            )
            flist[pl.ds((v + 1) * 8 + q, 1), :] = found
    for q in range(FCH):
        at = lane + q * BLK
        found = sum(
            jnp.sum(jnp.where(place[c] == at, tile_c[c], 0), axis=0, keepdims=True) for c in chunks
        )
        flist[pl.ds(q, 1), :] = found
        starts = sum(
            jnp.sum(
                jnp.where(
                    (place[c] == at)
                    & (tile_c[c] == jnp.sum(jnp.where(row_c[c] == lane, row_begin, 0), axis=1, keepdims=True)),
                    1, 0,
                ),
                axis=0, keepdims=True,
            )
            for c in chunks
        )
        flist[pl.ds(32 + q, 1), :] = starts

    await_arrival(tabs.at[pl.ds(0, 9)], tab_r.at[0])
    tabs_cp = pltpu.make_async_copy(tabs, tabs_sm, sm_sem.at[0])
    tabs_cp.start()
    tabs_cp.wait()

    def pack(v, db, dc, dst, base):
        at = reader(v, db, dc)
        for d in range(1 if db else 0, 4):
            for k in range(2):
                j = tabs_sm[v * 4 + d, 0, at + k * 64]
                dst[base + d * 2 + k] = ag[v][d * NB + j]

    def pass_on(v, b, dc):
        send(
            x[v].at[pl.ds(X_HOP + (dc * 4 + b) * 8, 8)],
            x[v].at[pl.ds(X_END + ((4 - dc - 1) * 4 + b) * 8, 8)],
            s3_s.at[v], s3_r.at[v], peer(v, 2, dc),
        )

    for v in range(NVAR):
        await_arrival(ag[v].at[pl.ds(NB, 3 * NB)], s1_r.at[v])
        for dc in (1, 3, 2, 0):
            pack(v, 0, dc, x[v], X_HOP + dc * 32)
            if dc:
                pass_on(v, 0, dc)
            for db in OFFS:
                base = (db * 4 + dc) * 8
                pack(v, db, dc, y[v], base)
                hop(v, db, dc, 2, 6)

    slot_c = [column(s) for s in slot_r]
    counts = [sum(jnp.sum(hits(s == lane + h * BLK), axis=0, keepdims=True) for s in slot_c) for h in range(2)]
    units = [lax.shift_right_logical(n + (BC - 1), BC.bit_length() - 1) for n in counts]
    units_c = [column(u) for u in units]
    firsts = [
        jnp.sum(jnp.where(sub < lane, units_c[0], 0), axis=0, keepdims=True),
        jnp.sum(jnp.where(sub < lane, units_c[1], 0) + units_c[0], axis=0, keepdims=True),
    ]
    for h in range(2):
        last = jnp.where(counts[h] > 0, firsts[h] + units[h] - 1, RUN_ZERO)
        ends[pl.ds(h, 1), :] = last
    order, place = [], []
    for c in chunks:
        before = sum(hits((slot_c[c] == slot_r[e]) & (lane + e * BLK < tile_c[c])) for e in chunks)
        order.append(jnp.sum(before, axis=1, keepdims=True))
        begin = jnp.sum(
            sum(jnp.where(slot_c[c] == lane + h * BLK, firsts[h], 0) for h in range(2)),
            axis=1, keepdims=True,
        )
        place.append(ones * (BC * begin + order[c]))
    start_c = [hits(o == 0) * ones for o in order]
    row_next = [r + 1 for r in row_c]
    for q in range(BCH):
        at = lane + q * BLK
        for base, what in ((0, tile_c), (8, row_next), (16, start_c)):
            found = sum(jnp.sum(jnp.where(place[c] == at, what[c], 0), axis=0, keepdims=True) for c in chunks)
            blist[pl.ds(base + q, 1), :] = found

    index1 = lax.broadcasted_iota(I32, (1, BLK), 1)
    for v in range(NVAR):
        k = lax.shift_right_logical(index1, 6)
        d, b, g = roles(v, digits(index1 & 63))
        own = Y_TWO + ((b - 1) * 4 + g) * 8 + k
        loc = jnp.where(b > 0, own, jnp.where(g > 0, Y_ONE + (g - 1) * 8 + k, k))
        loc_c = column(loc)
        for o in range(4):
            block = jnp.where(d == 0, tabs[v * 4 + o], 64)
            key = block * 128 + lane1
            block_c, key_c = column(block), column(key)
            rank = jnp.sum(hits(key_c < key), axis=0, keepdims=True)
            begin = jnp.sum(hits(block_c < block), axis=0, keepdims=True)
            rank_c, begin_c = column(rank), column(begin)
            value = loc_c + o * 2 + 512 * hits(rank_c == begin_c)
            found = jnp.sum(jnp.where(rank_c == lane, value, 0), axis=0, keepdims=True)
            upto = jnp.sum(hits(block_c <= lane), axis=0, keepdims=True)
            count = jnp.sum(hits(block_c == lane), axis=0, keepdims=True)
            rlist[pl.ds((v * 4 + o) * 2, 1), :] = found
            rlist[pl.ds((v * 4 + o) * 2 + 1, 1), :] = jnp.where(count > 0, upto - 1, 32)

    to_sm = [
        pltpu.make_async_copy(a, b, sm_sem.at[1 + i])
        for i, (a, b) in enumerate(((flist, flist_sm), (blist, blist_sm), (ends, ends_sm), (rlist, rlist_sm)))
    ]
    for cp in to_sm:
        cp.start()

    for v in range(NVAR):
        for dc in OFFS:
            await_arrival(x[v].at[pl.ds(X_HOP + (dc * 4 + 1) * 8, 24)], s2_r.at[v * 4 + dc])
            for b in (1, 3, 2):
                pass_on(v, b, dc)
    runs[RUN_ZERO] = jnp.zeros((BLK, BLK), BF16)
    gt[0] = jnp.zeros((BLK, BLK), BF16)
    for cp in to_sm:
        cp.wait()
    for v in range(NVAR):
        await_arrival(x[v].at[pl.ds(X_HOP + 8, 24)], s2_r.at[v * 4])
        await_arrival(x[v].at[pl.ds(X_END, 96)], s3_r.at[v])
    loads[2].wait()

    def forward_unit(u, acc):
        r, q = lax.div(u, 16), lax.rem(u, 16) * FC
        left, right = [], []
        for i in range(FC):
            left.append(w[flist_sm[r, q + i]])
            for v in range(NVAR):
                right.append(x[v][flist_sm[(v + 1) * 8 + r, q + i]])
        got = jnp.dot(
            jnp.concatenate(left, axis=1), jnp.concatenate(right, axis=0), preferred_element_type=F32
        )
        acc = jnp.where(flist_sm[32 + r, q] > 0, 0.0, acc) + got
        runs[u] = acc.astype(BF16)
        return acc

    lax.fori_loop(0, FU, forward_unit, jnp.zeros((BLK, BLK), F32), unroll=16)

    half, nodes_here = NB // 2, NB // 2 * BLK
    mine, theirs = feat * half, (1 - feat) * half
    for i in range(half):
        send_a[i] = runs[ends_sm[2, theirs + i]]
    send(send_a, full.at[feat], feat_s.at[0], feat_r.at[0], other)
    for cp in loads[:2]:
        cp.wait()
    for i in range(half):
        full[feat, i] = runs[ends_sm[2, mine + i]]
    await_arrival(full.at[1 - feat], feat_r.at[0])

    span = 3
    for i in range(0, half, span):
        nodes = pl.ds(i * BLK, span * BLK)
        left, right = (full[h, pl.ds(i, span)].reshape(span * BLK, BLK) for h in range(2))
        pre = jnp.dot(left, weight[0:BLK, :], preferred_element_type=F32)
        pre += jnp.dot(right, weight[BLK:, :], preferred_element_type=F32)
        sig = jax.nn.sigmoid(pre)
        hidden[nodes, :] = (pre * sig).astype(BF16)
        grad = (cot[nodes, :].astype(F32) * (sig * (1.0 + pre * (1.0 - sig)))).astype(BF16)
        grads[nodes, :] = grad
        for here in (False, True):
            rows = weight[pl.ds((feat if here else 1 - feat) * BLK, BLK), :]
            cols = lax.dot_general(rows, grad, (((1,), (1,)), ((), ())), preferred_element_type=F32).astype(BF16)
            for t in range(span):
                block = cols[:, t * BLK : (t + 1) * BLK]
                if here:
                    gt[1 + mine + i + t] = block
                else:
                    send_g[i + t] = block
            if not here:
                blocks = pl.ds(i, span)
                send(send_g.at[blocks], gt.at[pl.ds(1 + mine + i, span)], feat_s.at[1], feat_r.at[1], other)
    hidden_cp = pltpu.make_async_copy(hidden, hidden_hbm, in_sem.at[0])
    hidden_cp.start()
    await_arrival(gt.at[pl.ds(1 + theirs, half)], feat_r.at[1])

    def backward_unit(u, acc):
        r, q = lax.div(u, 64), lax.rem(u, 64) * BC
        left = [gt[blist_sm[8 + r, q + i]] for i in range(BC)]
        right = [w[blist_sm[r, q + i]] for i in range(BC)]
        got = jnp.dot(
            jnp.concatenate(left, axis=1), jnp.concatenate(right, axis=0), preferred_element_type=F32
        )
        acc = jnp.where(blist_sm[16 + r, q] > 0, 0.0, acc) + got
        runs[u] = acc.astype(BF16)
        return acc

    lax.fori_loop(0, BU, backward_unit, jnp.zeros((BLK, BLK), F32), unroll=39)

    for v in range(NVAR):
        await_arrival(y[v].at[pl.ds(32, 96)], s2_s.at[v])

    def fill(v, g, b):
        for d in range(4):
            t = turn[v]
            z = lax.rem(cz + jnp.where(t == 0, d, jnp.where(t == 1, g, b)), 4)
            xx = lax.rem(cx + jnp.where(t == 0, b, jnp.where(t == 1, d, g)), 4)
            yy = lax.rem(cy + jnp.where(t == 0, g, jnp.where(t == 1, b, d)), 4)
            slot = NB + (z * 16 + xx * 4 + yy) * 2
            for k in range(2):
                s = slot + k
                run = ends_sm[lax.div(s, BLK), lax.rem(s, BLK)]
                y[v][(g * 4 + b) * 8 + d * 2 + k] = runs[run, pl.ds(FIRST[v], ROWS[v])]

    def go_back(v, lam, kap):
        src = y[v].at[pl.ds(lam * 8, 8)] if kap == 0 else y[v].at[pl.ds(Y_ONE + (lam * 3 + kap - 1) * 8, 8)]
        send(
            src, y[v].at[pl.ds(Y_TWO + ((4 - lam - 1) * 4 + kap) * 8, 8)],
            b2_s.at[v], b2_r.at[v], peer(v, 1, lam),
        )

    for v in range(NVAR):
        for b in (1, 3, 2, 0):
            for g in OFFS:
                fill(v, g, b)
                send(
                    y[v].at[pl.ds((g * 4 + b) * 8, 8)],
                    y[v].at[pl.ds(Y_ONE + (b * 3 + (4 - g - 1)) * 8, 8)],
                    b3_s.at[v], b3_r.at[v * 4 + b], peer(v, 2, g),
                )
            fill(v, 0, b)
            if b:
                go_back(v, b, 0)

    for h in range(2):
        part = full[h].reshape(nodes_here, BLK)
        wt[h] = lax.dot_general(part, grads[...], (((0,), (0,)), ((), ())), preferred_element_type=F32)
    send(wt.at[1 - feat], wt_in, feat_s.at[2], feat_r.at[2], other)

    def gw_copy(n, src, dst, axis, off):
        send(src, dst, gw_s.at[n], gw_r.at[n], (moved(axis == 0, axis == 1, off), feat))

    def gw_step(n):
        if n == 0:
            await_arrival(wt_in, feat_r.at[2])
            wt[feat] = wt[feat] + wt_in[...]
            for off in OFFS:
                gw_copy(0, wt.at[feat, pl.ds(lax.rem(cz + off, 4) * 32, 32)], gw0.at[off], 0, off)
        elif n == 1:
            await_arrival(gw0.at[pl.ds(1, 3)], gw_r.at[0])
            gw0[0] = wt[feat, pl.ds(cz * 32, 32)] + gw0[1] + gw0[2] + gw0[3]
            for off in OFFS:
                gw_copy(1, gw0.at[0, pl.ds(lax.rem(cx + off, 4) * 8, 8)], gw1.at[off], 1, off)
        elif n == 2:
            await_arrival(gw1.at[pl.ds(1, 3)], gw_r.at[1])
            gw2[cy] = gw0[0, pl.ds(cx * 8, 8)] + gw1[1] + gw1[2] + gw1[3]
            for off in OFFS:
                gw_copy(2, gw2.at[cy], gw2.at[cy], 2, off)
        elif n == 3:
            await_arrival(gw1.at[pl.ds(1, 3)], gw_r.at[2])
            scale = float(64 * NB * BLK) ** (-0.5)
            gw3[cz, pl.ds(cx * 8, 8)] = (gw2[0] + gw2[1] + gw2[2] + gw2[3]) * scale
            for off in OFFS:
                gw_copy(3, gw3.at[cz, pl.ds(cx * 8, 8)], gw3.at[cz, pl.ds(cx * 8, 8)], 1, off)
        else:
            await_arrival(gw1.at[pl.ds(1, 3)], gw_r.at[3])
            for off in OFFS:
                gw_copy(4, gw3.at[cz], gw3.at[cz], 0, off)

    for v in range(NVAR):
        for b in (1, 3, 2):
            await_arrival(y[v].at[pl.ds(Y_ONE + b * 24, 24)], b3_r.at[v * 4 + b])
            for kap in (3, 1, 2):
                go_back(v, b, kap)
        gw_step(v)

    for v in range(NVAR):
        n = ROWS[v]
        await_arrival(y[v].at[pl.ds(Y_ONE, 24)], b3_r.at[v * 4])
        await_arrival(y[v].at[pl.ds(Y_TWO, 96)], b2_r.at[v])
        for o in (1, 3, 2, 0):
            r = (v * 4 + o) * 2

            def add(q, acc, v=v, r=r):
                code = rlist_sm[r, q]
                acc = jnp.where(code >= 512, 0.0, acc) + y[v][jnp.minimum(code & 511, Y_SIZE - 1)].astype(F32)
                rr[v][q] = acc.astype(BF16)
                return acc

            lax.fori_loop(0, 32, add, jnp.zeros((n, BLK), F32), unroll=4)
            rr[v][32] = jnp.zeros((n, BLK), BF16)
            for j in range(NB):
                ag[v][o * NB + j] = rr[v][rlist_sm[r + 1, j]]
            if o:
                send(
                    ag[v].at[pl.ds(o * NB, NB)], vin[v].at[pl.ds((4 - o - 1) * NB, NB)],
                    b1_s.at[v], b1_r.at[v], peer(v, 0, o),
                )
        if v < 2:
            gw_step(3 + v)

    for v in range(NVAR):
        await_arrival(vin[v], b1_r.at[v])
    for j in range(NB):
        run = ends_sm[0, j]
        parts = []
        for v in range(NVAR):
            total = runs[run, pl.ds(FIRST[v], ROWS[v])].astype(F32) + ag[v][j].astype(F32)
            for off in range(3):
                total += vin[v][off * NB + j].astype(F32)
            parts.append(total)
        grad_out[pl.ds(j * BLK, BLK), :] = jnp.transpose(jnp.concatenate(parts, axis=0)).astype(BF16)

    await_arrival(gw0.at[pl.ds(1, 3)], gw_r.at[4])
    for z in range(4):
        gw_out[pl.ds(z * 32, 32), :] = gw3[z]

    hidden_cp.wait()
    await_arrival(tabs.at[pl.ds(0, 9)], tab_s.at[0])
    await_arrival(send_a, feat_s.at[0])
    await_arrival(send_g, feat_s.at[1])
    await_arrival(wt_in, feat_s.at[2])
    for v in range(NVAR):
        await_arrival(ag[v].at[pl.ds(NB, 3 * NB)], s1_s.at[v])
        await_arrival(x[v].at[pl.ds(X_HOP + 32, 96)], s3_s.at[v])
        await_arrival(y[v].at[pl.ds(32, 96)], b3_s.at[v])
        await_arrival(y[v].at[pl.ds(Y_TWO, 96)], b2_s.at[v])
        await_arrival(ag[v].at[pl.ds(NB, 3 * NB)], b1_s.at[v])
    for n, ref in enumerate((gw0, gw1, gw1, gw1, gw0)):
        await_arrival(ref.at[pl.ds(1, 3)], gw_s.at[n])


def hand_over(*refs):
    n = (len(refs) - 1) // 3
    sem = refs[-1]
    inward = [pltpu.make_async_copy(refs[i], refs[2 * n + i], sem.at[i]) for i in range(n)]
    outward = [pltpu.make_async_copy(refs[2 * n + i], refs[n + i], sem.at[n + i]) for i in range(n)]
    for cp in inward:
        cp.start()
    for a, b in zip(inward, outward):
        a.wait()
        b.start()
    for cp in outward:
        cp.wait()


def local(features, tile_weights, tile_rows, tile_slots, send_blocks, weight, cotangent):
    dma = lambda n: pltpu.SemaphoreType.DMA((n,))
    vmem = lambda *shape, dtype=BF16: pltpu.VMEM(shape, dtype)
    smem = lambda *shape: pltpu.SMEM(shape, I32)
    in_vmem = pl.BlockSpec(memory_space=pltpu.VMEM)
    anywhere = pl.BlockSpec(memory_space=pl.ANY)
    nodes = NB * BLK
    scratch = [
        vmem(TILES, BLK, BLK),
        *[vmem(X_SIZE, n, BLK) for n in ROWS],
        *[vmem(Y_SIZE, n, BLK) for n in ROWS],
        *[vmem(4 * NB, n, BLK) for n in ROWS],
        *[vmem(3 * NB, n, BLK) for n in ROWS],
        *[vmem(33, n, BLK) for n in ROWS],
        vmem(BU + 1, BLK, BLK),
        vmem(12, 1, BLK, dtype=I32), smem(12, 1, BLK), smem(1, BLK),
        vmem(40, BLK, dtype=I32), smem(40, BLK),
        vmem(24, BLK, dtype=I32), smem(24, BLK),
        vmem(8, BLK, dtype=I32), smem(8, BLK),
        vmem(24, BLK, dtype=I32), smem(24, BLK),
        vmem(256, 256), vmem(nodes // 2, 256), vmem(nodes // 2, 256), vmem(nodes // 2, 256),
        vmem(NB, BLK, BLK), vmem(5, BLK, dtype=I32), vmem(5, BLK, dtype=I32), vmem(2, 64, dtype=I32), vmem(1, BLK, dtype=I32),
        vmem(2, NB // 2, BLK, BLK), vmem(NB // 2, BLK, BLK), vmem(NB + 1, BLK, BLK), vmem(NB // 2, BLK, BLK),
        vmem(2, BLK, 256, dtype=F32), vmem(BLK, 256, dtype=F32),
        vmem(4, 32, 256, dtype=F32), vmem(4, 8, 256, dtype=F32), vmem(4, 8, 256, dtype=F32),
        vmem(4, 32, 256, dtype=F32),
        dma(7), dma(6), dma(3), dma(3), dma(1), dma(1),
        dma(3), dma(3), dma(3), dma(12), dma(3), dma(3),
        dma(3), dma(12), dma(3), dma(3), dma(3), dma(3), dma(5), dma(5),
    ]
    out_shape = (
        jax.ShapeDtypeStruct((nodes // 2, 256), BF16),
        jax.ShapeDtypeStruct((nodes, BLK), BF16),
        jax.ShapeDtypeStruct((BLK, 256), F32),
    )
    results = pl.pallas_call(
        body,
        out_shape=out_shape,
        in_specs=[anywhere] * 7,
        out_specs=(anywhere, in_vmem, in_vmem),
        scratch_shapes=scratch,
        compiler_params=pltpu.CompilerParams(
            collective_id=0, has_side_effects=True, vmem_limit_bytes=64 * 2**20 - 2**16
        ),
        cost_estimate=pl.CostEstimate(flops=6 * 10**9, bytes_accessed=24 * 2**20, transcendentals=400000),
    )(
        features.reshape(NB, BLK, BLK), tile_weights, tile_rows.reshape(5, BLK), tile_slots.reshape(5, BLK),
        jnp.swapaxes(send_blocks, 1, 2).reshape(2, 64), weight, cotangent,
    )
    return pl.pallas_call(
        hand_over,
        out_shape=out_shape,
        in_specs=[anywhere] * 3,
        out_specs=(anywhere,) * 3,
        scratch_shapes=[*[pltpu.VMEM(o.shape, o.dtype) for o in out_shape], dma(6)],
    )(*results)


def solution(mesh):
    placed = (
        P("dom", "feat"),
        P("dom", None, None),
        P("dom"),
        P("dom"),
        P("dom", None, None),
        P(),
        P(("dom", "feat"), None),
    )
    return jax.shard_map(
        local,
        mesh=mesh,
        in_specs=placed,
        out_specs=(P(("dom", "feat"), None), P("dom", "feat"), P("feat", None)),
        check_vma=False,
    )
```
